128 devices in a mesh: group: 4 (over y), shard: 32 (over z, x, core).
Axes of the slice: x: 4, y: 4, z: 4, core: 2. Of those that a mesh axis runs over, the one named last changes fastest.
Arguments:
- tokens: bfloat16 [128, 192, 768], P(('group', 'shard')), may hold values from -650 to 650
- norm_gain: float32 [768], replicated, may hold values from 0.1 to 1.9
- w_query: bfloat16 [768, 768], P('shard'), may hold values from -8 to 8
- w_key: bfloat16 [768, 768], P('shard'), may hold values from -0.21875 to 0.21875
- w_value: bfloat16 [768, 768], P('shard'), may hold values from -0.625 to 0.625
- w_out: bfloat16 [768, 768], P('shard'), may hold values from -0.21875 to 0.21875
- owner_map: int32 [4, 32], P('group'), may hold values from 0 to 31, each once within a row
- pair_images: int32 [1024, 2], P(('group', 'shard')), may hold values from 0 to 31, as said below
- pair_count: int32 [128], P(('group', 'shard')), may hold values from 1 to 8, 512 in all
- confidence: int32 [1024, 2], P(('group', 'shard')), may hold values from 1 to 8
Outputs:
- updated: bfloat16 [128, 192, 768], P(('group', 'shard'))
The draws below stay inside these ranges and needn't reach their ends.
Inputs may be any that keep to these rules, and one draw needn't show every extreme that they name: `pair_images`: each row names two different images of the listing device's own group, by their index within that group. Device d lists its pairs in its first pair_count[d] rows of pair_images and confidence; the other rows are unused.
All inputs are finite; a program needn't handle non-finite values.
Results may differ from the reference program's by a relative error of at most 0.013.
The reference program's roundings to bfloat16 on the way (of `normed`, `query`, `attention` and `attended`) count: a program that leaves them out, or rounds other values in their place, can miss the bound.
Values may be sent and summed in bfloat16 or wider, within the bound.
A program may use at most 128 MiB of HBM per device.

```python
import math
import jax
import jax.numpy as jnp
import numpy as np
from jax import lax

D = 768
HEADS = 12
HEAD_DIM = 64
SEQ = 192
PAIR_CAP = 8
IMAGES = 128
SLOTS = 1024
PAIRS = 512
N_GROUP = 4
N_SHARD = 32
DEVICES = 128


def draw_tokens(key, part):
    first = jax.random.fold_in(jax.random.fold_in(key, 11), 0)
    values = jnp.clip(jax.random.normal(first, (IMAGES, SEQ, D), jnp.float32), -6.0, 6.0)
    return values.astype(jnp.bfloat16)


def draw_w_query(key, part):
    values = jax.random.normal(jax.random.fold_in(key, 23), (D, D), jnp.float32) * D ** (-0.5)
    return jnp.clip(values, -8.0, 8.0).astype(jnp.bfloat16)


def draw_pair_images(key, part):
    first, second = jax.random.split(jax.random.fold_in(key, 37))
    left = jax.random.randint(first, (SLOTS, 1), 0, N_SHARD, dtype=jnp.int32)
    offset = jax.random.randint(second, (SLOTS, 1), 1, N_SHARD, dtype=jnp.int32)
    return jnp.concatenate([left, (left + offset) % N_SHARD], axis=1)


def plant(values, stream_key, smallest, high):
    longest = values.shape.index(max(values.shape))
    spots = []
    for shift in (0, 1):
        where = [jax.random.randint(jax.random.fold_in(stream_key, axis), (), 0, length) for axis, length in enumerate(values.shape)]
        where[longest] = (where[longest] + shift) % values.shape[longest]
        spots.append(tuple(where))
    return values.at[spots[0]].set(smallest).at[spots[1]].set(high)


def level_of(own_key, extent, shards, smallest, largest):
    level = 1.0
    for position, parts in shards:
        steps = jax.random.uniform(jax.random.fold_in(jax.random.fold_in(own_key, 6), position), (parts,), jnp.float32, smallest / len(shards), largest / len(shards))
        level = level * jnp.repeat(jnp.exp(steps), extent[position] // parts).reshape((-1,) + (1,) * (len(extent) - 1 - position))
    return level


def split_up(number_of, total, limit, slope):
    weights = [(1 << 20) // math.isqrt(standing ** slope) + 1 for standing in range(2, number_of + 1)]
    spare, holding = total - limit - (number_of - 1), [1] * (number_of - 1)
    while spare > 0:
        free = [i for i in range(number_of - 1) if holding[i] < limit]
        pool, left = sum([weights[i] for i in free]), spare
        for i in free:
            addition = min(limit - holding[i], max(1, left * weights[i] // pool), spare)
            holding[i] = holding[i] + addition
            spare = spare - addition
    return np.array([limit] + holding)


def uneven(rng, number_of, total, most, lean):
    if number_of == 2:
        one = jax.random.randint(rng, (), max(1, total - most), min(most, total - 1) + 1)
        return jnp.stack([one, total - one])
    tallies = jnp.asarray(split_up(number_of, total, most, lean), jnp.int32)
    pairs = (number_of - 1) // 2
    source_of, receiver = tallies[1:1 + 2 * pairs:2], tallies[2:2 + 2 * pairs:2]
    slack = jnp.minimum(source_of - 1, most - receiver)
    shifted = jax.random.randint(jax.random.fold_in(rng, 1), (pairs,), 0, 1 << 20) % (slack + 1)
    tallies = tallies.at[1:1 + 2 * pairs:2].set(source_of - shifted).at[2:2 + 2 * pairs:2].set(receiver + shifted)
    return tallies[jax.random.permutation(jax.random.fold_in(rng, 2), number_of)]


def noise(own_key, extent, deviation, limit, cuts=(), kind=jnp.bfloat16):
    entries = jax.random.normal(own_key, extent, jnp.float32) * deviation
    if len(cuts) > 0:
        entries = level_of(own_key, extent, cuts, -0.22, 0.18) * entries
    return jnp.clip(entries, min=-limit, max=limit).astype(kind)


def setup_inputs(seed: int = 0) -> dict:
    key_list = jax.random.split(jax.random.key(seed), 11)
    return {
        "tokens": draw_tokens(jax.random.fold_in(key_list[10], 71), 0),
        "norm_gain": jnp.clip(1.0 + 0.18 * jax.random.normal(key_list[1], (D,), jnp.float32), 0.1, 1.9),
        "w_query": draw_w_query(jax.random.fold_in(key_list[10], 71), 0),
        "w_key": noise(key_list[3], (D, D), D ** -0.5, 0.21875, ((0, 32),)),
        "w_value": noise(key_list[4], (D, D), (D // 9) ** -0.5, 0.625, ((0, 32),)),
        "w_out": noise(key_list[5], (D, D), D ** -0.5, 0.21875, ((0, 32),)),
        "owner_map": jax.vmap(lambda own: jax.random.permutation(own, N_SHARD))(jax.random.split(key_list[6], N_GROUP)).reshape((N_GROUP, N_SHARD)).astype(jnp.int32),
        "pair_images": draw_pair_images(jax.random.fold_in(key_list[10], 71), 0),
        "pair_count": uneven(key_list[8], DEVICES, PAIRS, PAIR_CAP, 2).astype(jnp.int32),
        "confidence": plant(jax.random.randint(key_list[9], (SLOTS, 2), 1, 9), jax.random.fold_in(key_list[9], 1), 1, 8).astype(jnp.int32),
    }


def layer_norm(values, norm_gain):
    values = values.astype(jnp.float32)
    average = lax.optimization_barrier(jnp.mean(values, axis=-1, keepdims=True))
    centred = values - average
    variance = lax.optimization_barrier(jnp.mean(centred * centred, axis=-1, keepdims=True))
    return (centred * lax.rsqrt(variance + 1e-05) * norm_gain).astype(jnp.bfloat16)

def attend(query_rows, key_rows, value_rows, w_out):
    length = query_rows.shape[0]
    query_heads = query_rows.reshape(length, HEADS, HEAD_DIM).astype(jnp.float32)
    key_heads = key_rows.reshape(length, HEADS, HEAD_DIM).astype(jnp.float32)
    value_heads = value_rows.reshape(length, HEADS, HEAD_DIM).astype(jnp.float32)
    scores = jnp.einsum('qhd,khd->hqk', query_heads, key_heads) * (1.0 / math.sqrt(HEAD_DIM))
    scores = scores - lax.optimization_barrier(jnp.max(scores, axis=-1, keepdims=True))
    expo = jnp.exp(scores)
    attention = (expo / lax.optimization_barrier(jnp.sum(expo, axis=-1, keepdims=True))).astype(jnp.bfloat16)
    attended = jnp.einsum('hqk,khd->qhd', attention.astype(jnp.float32), value_heads)
    attended = attended.reshape(length, HEADS * HEAD_DIM).astype(jnp.bfloat16)
    return jnp.dot(attended, w_out, preferred_element_type=jnp.float32)

def reference(tokens, norm_gain, w_query, w_key, w_value, w_out, owner_map, pair_images, pair_count, confidence):
    normed = layer_norm(tokens, norm_gain)
    flat_rows = normed.reshape(IMAGES * SEQ, D)
    query = jnp.dot(flat_rows, w_query, preferred_element_type=jnp.float32).astype(jnp.bfloat16).reshape(IMAGES, SEQ, D)
    key_all = jnp.dot(flat_rows, w_key, preferred_element_type=jnp.float32).astype(jnp.bfloat16).reshape(IMAGES, SEQ, D)
    value_all = jnp.dot(flat_rows, w_value, preferred_element_type=jnp.float32).astype(jnp.bfloat16).reshape(IMAGES, SEQ, D)
    slot_ids = jnp.arange(SLOTS, dtype=jnp.int32)
    device_ids = slot_ids // PAIR_CAP
    group_ids = device_ids // N_SHARD
    usable = slot_ids % PAIR_CAP < pair_count[device_ids]
    store_first = (group_ids * N_SHARD + owner_map[group_ids, pair_images[:, 0]]).astype(jnp.int32)
    store_second = (group_ids * N_SHARD + owner_map[group_ids, pair_images[:, 1]]).astype(jnp.int32)
    weight_first = jnp.where(usable, confidence[:, 0], 0).astype(jnp.float32)
    weight_second = jnp.where(usable, confidence[:, 1], 0).astype(jnp.float32)

    def advance(carried, element):
        numerator, weight_total = carried
        first, second, first_weight, second_weight = element
        first_out = attend(query[first], key_all[second], value_all[second], w_out)
        second_out = attend(query[second], key_all[first], value_all[first], w_out)
        numerator = numerator.at[first].add(first_weight * first_out)
        numerator = numerator.at[second].add(second_weight * second_out)
        weight_total = weight_total.at[first].add(first_weight)
        weight_total = weight_total.at[second].add(second_weight)
        return ((numerator, weight_total), None)
    start = (jnp.zeros((IMAGES, SEQ, D), jnp.float32), jnp.zeros((IMAGES,), jnp.float32))
    (numerator, weight_total), _ = lax.scan(advance, start, (store_first, store_second, weight_first, weight_second))
    return (numerator / (1.0 + weight_total)[:, None, None]).astype(jnp.bfloat16)
```

```python
import math

import jax
import jax.numpy as jnp
from jax import lax
from jax.experimental import pallas as pl
from jax.experimental.pallas import tpu as pltpu
from jax.sharding import PartitionSpec as P

MESH = pl.DeviceIdType.MESH
F32, BF16, I32 = jnp.float32, jnp.bfloat16, jnp.int32
SEQ, D, RING, PLANE = 192, 768, 4, 16
WIDE = 192
ROWS = 24
NT = (((1,), (1,)), ((), ()))
TN = (((0,), (0,)), ((), ()))
FIRST = (0, 3, 1, 2)


def place():
    shard = lax.axis_index("shard")
    core = lax.rem(shard, 2)
    chip = lax.div(shard, 2)
    return lax.rem(chip, RING), lax.div(chip, RING), core


def device(x, z, core):
    return {"shard": (z * RING + x) * 2 + core}


def gather_kernel(
    tok, gain, wq, wk, wv, wo, omap, pimg, pcnt, conf,
    kv, qt, weights, total, wo_all,
    img, staged, wplane, woplane, lists, wt, send, recv, pair_send, pair_recv,
):
    x, z, core = place()
    chip = z * RING + x

    def turn(value, offset):
        return lax.rem(value + offset, RING)

    def slot(ox, oz):
        return turn(z, oz) * RING + turn(x, ox)

    sibling = device(x, z, 1 - core)
    barrier = pltpu.get_barrier_semaphore()
    for offset in (1, 2, 3):
        pl.semaphore_signal(barrier, 1, device_id=device(turn(x, offset), z, core), device_id_type=MESH)
        pl.semaphore_signal(barrier, 1, device_id=device(x, turn(z, offset), core), device_id_type=MESH)
    pl.semaphore_signal(barrier, 1, device_id=sibling, device_id_type=MESH)

    parts = [w[...].astype(F32) for w in (wq, wk, wv)]
    for g in range(RING):
        cols = [w[:, g * WIDE:(g + 1) * WIDE] for w in parts] + [jnp.zeros((ROWS, 64), F32)]
        slice_g = jnp.concatenate(cols, axis=1)
        staged[g] = jnp.concatenate([slice_g, jnp.zeros((8, 640), F32)], axis=0).astype(BF16)
    wplane[core, chip] = staged[x]
    woplane[core, chip] = jnp.concatenate(
        [wo[...].astype(F32), jnp.zeros((8, D), F32)], axis=0
    ).astype(BF16)
    lane32 = lax.broadcasted_iota(I32, (8, 32), 1)

    def stored(column):
        return jnp.sum(jnp.where(pimg[:, column:column + 1] == lane32, omap[...], 0), axis=1, keepdims=True)

    lane = lax.broadcasted_iota(I32, (8, 128), 1)
    listed = lax.broadcasted_iota(I32, (8, 128), 0) < pcnt[...]
    lists[core, chip] = jnp.where(
        lane == 0, stored(0),
        jnp.where(
            lane == 1, stored(1),
            jnp.where(
                lane == 2, jnp.where(listed, conf[:, 0:1], 0),
                jnp.where(lane == 3, jnp.where(listed, conf[:, 1:2], 0), 0),
            ),
        ),
    )
    values = tok[0].astype(F32)
    centred = values - jnp.mean(values, axis=-1, keepdims=True)
    variance = jnp.mean(centred * centred, axis=-1, keepdims=True)
    img[chip] = (centred * lax.rsqrt(variance + 1e-05) * gain[...]).astype(BF16)

    pl.semaphore_wait(barrier, 7)

    started = []

    def copy(source, target, number, where):
        return pltpu.make_async_remote_copy(
            src_ref=source, dst_ref=target, send_sem=send.at[number], recv_sem=recv.at[number],
            device_id=where, device_id_type=MESH,
        )

    def start(source, target, number, where):
        one = copy(source, target, number, where)
        one.start()
        started.append(one)

    def arrived(target, number):
        copy(target, target, number, sibling).wait_recv()

    def along_x(buffer, base, outgoing=None):
        for offset in (1, 2, 3):
            block = buffer.at[core, chip]
            source = block if outgoing is None else outgoing.at[turn(x, offset)]
            start(source, block, base + offset - 1, device(turn(x, offset), z, core))

    def along_z(buffer, base):
        for offset in (1, 2, 3):
            arrived(buffer.at[core, z * RING + turn(x, 4 - offset)], base + offset - 1)
        for offset in (1, 2, 3):
            row = buffer.at[core, pl.ds(z * RING, RING)]
            start(row, row, base + 2 + offset, device(x, turn(z, offset), core))

    def across(buffer, base):
        for offset in (1, 2, 3):
            arrived(buffer.at[core, pl.ds(turn(z, 4 - offset) * RING, RING)], base + 2 + offset)
        start(buffer.at[core], buffer.at[core], base + 6, sibling)

    def ended(buffer, base):
        arrived(buffer.at[1 - core], base + 6)

    def piece(half, first, second, part=None):
        low, count = (96 * half, 96) if part is None else (96 * half + 48 * part, 48)
        where = slot(first, second) if half == 0 else slot(second, first)
        return img.at[where, pl.ds(low, count)]

    def neighbour(axis, direction):
        step = 1 if direction == 0 else 3
        return device(turn(x, step), z, core) if axis == 0 else device(x, turn(z, step), core)

    def first_ring(half, direction):
        start(piece(half, 0, 0), piece(half, 0, 0), 20 * half + direction, neighbour(half, direction))

    def first_forward(half, direction):
        block = piece(half, (3, 1)[direction], 0, direction)
        start(block, block, 20 * half + 2 + direction, neighbour(half, direction))

    def second_ring(half, k):
        for direction in (0, 1):
            block = piece(half, FIRST[k], 0)
            start(block, block, 20 * half + 4 + 4 * k + direction, neighbour(1 - half, direction))

    def second_forward(half, k, direction):
        block = piece(half, FIRST[k], (3, 1)[direction], direction)
        start(block, block, 20 * half + 6 + 4 * k + direction, neighbour(1 - half, direction))

    def got_first(half, direction):
        arrived(piece(half, (3, 1)[direction], 0), 20 * half + direction)

    def got_first_forward(half, direction):
        arrived(piece(half, 2, 0, direction), 20 * half + 2 + direction)

    def got_second(half, k, direction):
        arrived(piece(half, FIRST[k], (3, 1)[direction]), 20 * half + 4 + 4 * k + direction)

    def got_second_forward(half, k, direction):
        arrived(piece(half, FIRST[k], 2, direction), 20 * half + 6 + 4 * k + direction)

    def pair_copy(where, row):
        return pltpu.make_async_remote_copy(
            src_ref=kv.at[row], dst_ref=kv.at[row], send_sem=pair_send.at[where],
            recv_sem=pair_recv.at[where], device_id=sibling, device_id_type=MESH,
        )

    def project(count, offsets):
        def one(i, carried):
            where = slot(*offsets(i))
            row = where * 2 + core
            normed = img[where]
            kv[row, 0:WIDE, :] = lax.dot_general(
                normed, wt[WIDE:2 * WIDE, :], NT, preferred_element_type=F32
            ).astype(BF16)
            kv[row, WIDE:2 * WIDE, :] = lax.dot_general(
                wt[2 * WIDE:3 * WIDE, :], normed, NT, preferred_element_type=F32
            ).astype(BF16)
            pair_copy(where, row).start()
            return carried

        lax.fori_loop(0, count, one, 0)

    W0, L0, O0 = 40, 47, 54
    along_x(wplane, W0, staged)
    along_x(lists, L0)
    for half in (0, 1):
        for direction in (0, 1):
            first_ring(half, direction)
        second_ring(half, 0)
    along_z(wplane, W0)
    along_z(lists, L0)

    for direction in (0, 1):
        for half in (0, 1):
            got_first(half, direction)
            first_forward(half, direction)
            second_ring(half, 1 + direction)
    for direction in (0, 1):
        for half in (0, 1):
            got_second(half, 0, direction)
            second_forward(half, 0, direction)
    across(wplane, W0)
    across(lists, L0)
    along_x(woplane, O0)
    ended(wplane, W0)
    ended(lists, L0)

    for j in (0, 1):
        blocks = []
        for one in range(8 * j, 8 * j + 8):
            for c in (0, 1):
                blocks.append(wplane[c, one].astype(F32)[0:ROWS, :])
        wt[:, 384 * j:384 * (j + 1)] = jnp.concatenate(blocks, axis=0).T.astype(BF16)
    project(1, lambda i: (i, i))
    project(4, lambda i: ((1 + 2 * (i % 2)) * (1 - i // 2), (1 + 2 * (i % 2)) * (i // 2)))

    table = lists[...].reshape(2 * PLANE * 8, 128)
    lanes = lax.broadcasted_iota(I32, (2 * PLANE * 8, 128), 1)
    first, second = table[:, 0:1], table[:, 1:2]
    one_weight, two_weight = table[:, 2:3], table[:, 3:4]
    at_first, at_second = first == lanes, second == lanes

    def weight_row(image):
        taken = jnp.where(at_second, jnp.where(first == image, one_weight, 0), 0)
        taken = taken + jnp.where(at_first, jnp.where(second == image, two_weight, 0), 0)
        return jnp.sum(taken, axis=0, keepdims=True)

    rows = [weight_row((z * RING + i) * 2 + core) for i in range(RING)]
    weights[...] = jnp.concatenate(rows + [jnp.zeros((4, 128), I32)], axis=0)
    own = jnp.sum(weight_row(chip * 2 + core).astype(F32), axis=1, keepdims=True)
    total[...] = jnp.broadcast_to(1.0 + own, (8, 128))

    for half in (0, 1):
        for direction in (0, 1):
            got_first_forward(half, direction)
        second_ring(half, 3)
    for k in (1, 2):
        for direction in (0, 1):
            for half in (0, 1):
                got_second(half, k, direction)
                second_forward(half, k, direction)
    for half in (0, 1):
        for direction in (0, 1):
            got_second_forward(half, 0, direction)
    along_z(woplane, O0)
    project(4, lambda i: (1 + 2 * (i // 2), 1 + 2 * (i % 2)))
    project(2, lambda i: (2 * (1 - i), 2 * i))

    def one_query(i, carried):
        qt[i] = lax.dot_general(
            wt[0:WIDE, :], img[z * RING + i], NT, preferred_element_type=F32
        ).astype(BF16)
        return carried

    lax.fori_loop(0, RING, one_query, 0)

    for direction in (0, 1):
        for half in (0, 1):
            got_second(half, 3, direction)
            second_forward(half, 3, direction)
    for k in (1, 2):
        for direction in (0, 1):
            for half in (0, 1):
                got_second_forward(half, k, direction)
    across(woplane, O0)
    project(4, lambda i: (
        2 * (1 - i // 2) + (1 + 2 * (i % 2)) * (i // 2),
        (1 + 2 * (i % 2)) * (1 - i // 2) + 2 * (i // 2),
    ))
    for half in (0, 1):
        for direction in (0, 1):
            got_second_forward(half, 3, direction)
    project(1, lambda i: (i + 2, i + 2))
    ended(woplane, O0)
    for one in range(PLANE):
        blocks = [woplane[c, one].astype(F32)[0:ROWS, :] for c in (0, 1)]
        wo_all[2 * ROWS * one:2 * ROWS * (one + 1), :] = jnp.concatenate(blocks, axis=0).astype(BF16)

    for one in started:
        one.wait_send()

    def drain(where, carried):
        pair_copy(where, where * 2 + core).wait_send()
        pair_copy(where, where * 2 + 1 - core).wait_recv()
        return carried

    lax.fori_loop(0, PLANE, drain, 0)


WINDOWS = ((0, 256, 0), (128, 384, 64), (384, 576, 0))


def attend_kernel(weights, kv, qt, out, masked, acc, chosen, chosen_weight):
    for i in range(RING):
        masked[i] = jnp.zeros((WIDE, 3 * SEQ), BF16)
        for h in range(3):
            masked[i, 64 * h:64 * (h + 1), SEQ * h:SEQ * (h + 1)] = qt[i, 64 * h:64 * (h + 1), :]
    acc[...] = jnp.zeros_like(acc)

    def note(number, count):
        weight = weights[number // 32, number % 32]
        chosen[count] = number
        chosen_weight[count] = weight
        return count + jnp.where(weight > 0, 1, 0)

    count = lax.fori_loop(0, 128, note, 0, unroll=8)
    chosen[count] = 0
    chosen_weight[count] = 0
    factor = math.log2(math.e) / 8.0

    def direction(entry):
        number = chosen[entry]
        i, t = number // 32, number % 32
        weight = chosen_weight[entry].astype(F32)
        scores = jnp.dot(kv[t, 0:WIDE, :], masked[i], preferred_element_type=F32)
        top = jnp.max(scores, axis=0, keepdims=True)
        expo = jnp.exp2((scores - top) * factor)
        scale = 1.0 / jnp.sum(expo, axis=0, keepdims=True)
        expo = expo.astype(BF16)
        for h, (low, high, _) in enumerate(WINDOWS):
            one = jnp.dot(
                kv[t, WIDE + 64 * h:WIDE + 64 * (h + 1), :], expo[:, low:high],
                preferred_element_type=F32,
            )
            one = (one * scale[:, low:high]).astype(BF16).astype(F32) * weight
            acc[i, h, :, 0:high - low] += one

    def two(number, carried):
        direction(2 * number)
        direction(2 * number + 1)
        return carried

    lax.fori_loop(0, (count + 1) // 2, two, 0)
    for i in range(RING):
        for h, (_, _, low) in enumerate(WINDOWS):
            out[i, 64 * h:64 * (h + 1), :] = acc[i, h][:, low:low + SEQ].astype(BF16)


def output_kernel(attended, wo_all, total, out, held, send, recv):
    x, z, core = place()
    barrier = pltpu.get_barrier_semaphore()
    for offset in (1, 2, 3):
        pl.semaphore_signal(
            barrier, 1, device_id=device(lax.rem(x + offset, RING), z, core), device_id_type=MESH
        )
    pl.semaphore_wait(barrier, 3)
    copies = []
    for offset in (1, 2, 3):
        peer = lax.rem(x + offset, RING)
        one = pltpu.make_async_remote_copy(
            src_ref=attended.at[peer], dst_ref=held.at[x], send_sem=send.at[offset - 1],
            recv_sem=recv.at[offset - 1], device_id=device(peer, z, core), device_id_type=MESH,
        )
        one.start()
        copies.append(one)
    held[x] = attended[x]
    for offset in (1, 2, 3):
        peer = lax.rem(x + 4 - offset, RING)
        pltpu.make_async_remote_copy(
            src_ref=attended.at[peer], dst_ref=held.at[peer], send_sem=send.at[offset - 1],
            recv_sem=recv.at[offset - 1], device_id=device(peer, z, core), device_id_type=MESH,
        ).wait_recv()
    summed = held[...].reshape(D, SEQ)
    numerator = lax.dot_general(summed, wo_all[...], TN, preferred_element_type=F32)
    out[0] = (numerator / total[0:1, 0:1]).astype(BF16)
    for one in copies:
        one.wait_send()


VMEM = pl.BlockSpec(memory_space=pltpu.VMEM)
SMEM = pl.BlockSpec(memory_space=pltpu.SMEM)


def shards(tokens, norm_gain, w_query, w_key, w_value, w_out, owner_map, pair_images, pair_count, confidence):
    kv, qt, weights, total, wo_all = pl.pallas_call(
        gather_kernel,
        out_shape=(
            jax.ShapeDtypeStruct((2 * PLANE, 2 * WIDE, SEQ), BF16),
            jax.ShapeDtypeStruct((RING, WIDE, SEQ), BF16),
            jax.ShapeDtypeStruct((8, 128), I32),
            jax.ShapeDtypeStruct((8, 128), F32),
            jax.ShapeDtypeStruct((D, D), BF16),
        ),
        in_specs=[VMEM] * 10,
        out_specs=(VMEM,) * 5,
        scratch_shapes=[
            pltpu.VMEM((PLANE, SEQ, D), BF16),
            pltpu.VMEM((RING, 32, 640), BF16),
            pltpu.VMEM((2, PLANE, 32, 640), BF16),
            pltpu.VMEM((2, PLANE, 32, D), BF16),
            pltpu.VMEM((2, PLANE, 8, 128), I32),
            pltpu.VMEM((640, D), BF16),
            pltpu.SemaphoreType.DMA((61,)),
            pltpu.SemaphoreType.DMA((61,)),
            pltpu.SemaphoreType.DMA((PLANE,)),
            pltpu.SemaphoreType.DMA((PLANE,)),
        ],
        compiler_params=pltpu.CompilerParams(
            collective_id=0, has_side_effects=True, vmem_limit_bytes=48 * 1024 * 1024
        ),
        name="gather_project",
    )(
        tokens, norm_gain.reshape(1, D), w_query, w_key, w_value, w_out,
        owner_map, pair_images, pair_count.reshape(1, 1), confidence,
    )
    attended = pl.pallas_call(
        attend_kernel,
        out_shape=jax.ShapeDtypeStruct((RING, WIDE, SEQ), BF16),
        in_specs=[SMEM, VMEM, VMEM],
        out_specs=VMEM,
        scratch_shapes=[
            pltpu.VMEM((RING, WIDE, 3 * SEQ), BF16),
            pltpu.VMEM((RING, 3, 64, 256), F32),
            pltpu.SMEM((136,), I32),
            pltpu.SMEM((136,), I32),
        ],
        compiler_params=pltpu.CompilerParams(vmem_limit_bytes=48 * 1024 * 1024),
        name="attend",
    )(weights, kv, qt)
    return pl.pallas_call(
        output_kernel,
        out_shape=jax.ShapeDtypeStruct((1, SEQ, D), BF16),
        in_specs=[VMEM] * 3,
        out_specs=VMEM,
        scratch_shapes=[
            pltpu.VMEM((RING, WIDE, SEQ), BF16),
            pltpu.SemaphoreType.DMA((3,)),
            pltpu.SemaphoreType.DMA((3,)),
        ],
        compiler_params=pltpu.CompilerParams(
            collective_id=1, has_side_effects=True, vmem_limit_bytes=48 * 1024 * 1024
        ),
        name="exchange_output",
    )(attended, wo_all, total)


def solution(mesh):
    both = P(("group", "shard"))
    in_specs = (
        P(("group", "shard"), None, None),
        P(),
        P("shard", None),
        P("shard", None),
        P("shard", None),
        P("shard", None),
        P("group", None),
        P(("group", "shard"), None),
        both,
        P(("group", "shard"), None),
    )
    out_specs = P(("group", "shard"), None, None)
    return jax.shard_map(shards, mesh=mesh, in_specs=in_specs, out_specs=out_specs, check_vma=False)
```

```python
import math

import jax
import jax.numpy as jnp
from jax import lax
from jax.experimental import pallas as pl
from jax.experimental.pallas import tpu as pltpu
from jax.sharding import PartitionSpec as P

MESH = pl.DeviceIdType.MESH
F32, BF16, I32 = jnp.float32, jnp.bfloat16, jnp.int32
SEQ, D, RING, PLANE = 192, 768, 4, 16
WIDE = 192
ROWS = 24
NT = (((1,), (1,)), ((), ()))
TN = (((0,), (0,)), ((), ()))
FIRST = (0, 3, 1, 2)


def place():
    shard = lax.axis_index("shard")
    core = lax.rem(shard, 2)
    chip = lax.div(shard, 2)
    return lax.rem(chip, RING), lax.div(chip, RING), core


def device(x, z, core):
    return {"shard": (z * RING + x) * 2 + core}


def gather_kernel(
    tok_h, gain_h, wq_h, wk_h, wv_h, wo_h, omap_h, pimg_h, pcnt_h, conf_h,
    kv, both, third, weights, total, wo_all,
    tok, gain, wq, wk, wv, wo, omap, pimg, pcnt, conf,
    img, staged, wplane, woplane, lists, wt, load, send, recv, pair_send, pair_recv,
):
    x, z, core = place()
    y = lax.axis_index("group")
    chip = z * RING + x

    def turn(value, offset):
        return lax.rem(value + offset, RING)

    def slot(ox, oz):
        return turn(z, oz) * RING + turn(x, ox)

    sibling = device(x, z, 1 - core)
    loads = [
        pltpu.make_async_copy(source, target, load.at[n])
        for n, (source, target) in enumerate((
            (tok_h, tok), (gain_h, gain), (wq_h, wq), (wk_h, wk), (wv_h, wv), (wo_h, wo),
            (omap_h, omap), (pimg_h, pimg), (pcnt_h, pcnt), (conf_h, conf),
        ))
    ]
    for one in loads:
        one.start()
    barrier = pltpu.get_barrier_semaphore()
    for offset in (1, 2, 3):
        for peer in (device(turn(x, offset), z, core), device(x, turn(z, offset), core), {"group": turn(y, offset)}):
            pl.semaphore_signal(barrier, 1, device_id=peer, device_id_type=MESH)
    pl.semaphore_signal(barrier, 1, device_id=sibling, device_id_type=MESH)

    for one in loads:
        one.wait()
    values = tok[0].astype(F32)
    centred = values - jnp.mean(values, axis=-1, keepdims=True)
    variance = jnp.mean(centred * centred, axis=-1, keepdims=True)
    img[chip] = (centred * lax.rsqrt(variance + 1e-05) * gain[...].reshape(1, D)).astype(BF16)

    square = (lax.broadcasted_iota(I32, (32, 32), 0), lax.broadcasted_iota(I32, (32, 32), 1))
    owners = jnp.sum(jnp.where(square[0] == square[1], omap[...], 0), axis=1, keepdims=True)
    image = lax.broadcasted_iota(I32, (32, 8), 0)
    stored = [
        jnp.sum(jnp.where(pimg[r:r + 1, :] == image, owners, 0), axis=0, keepdims=True) for r in (0, 1)
    ]
    listed = lax.broadcasted_iota(I32, (2, 8), 1) < pcnt[0]
    entries = jnp.concatenate(stored + [jnp.where(listed, conf[...], 0), jnp.zeros((4, 8), I32)], axis=0)
    entries = jnp.concatenate([entries, jnp.zeros((8, 120), I32)], axis=1)
    lists[core, chip] = pltpu.roll(entries, 8 * chip, 1)

    @pl.when(x == y)
    def _():
        parts = [w[...].astype(F32) for w in (wq, wk, wv)]
        for g in range(RING):
            cols = [w[:, g * WIDE:(g + 1) * WIDE] for w in parts] + [jnp.zeros((ROWS, 64), F32)]
            staged[g] = jnp.concatenate(cols, axis=1).astype(BF16)
        wplane[core, y, z] = staged[x]
        woplane[core, y, z] = wo[...]

    pl.semaphore_wait(barrier, 10)

    started = []

    def copy(source, target, number, where):
        return pltpu.make_async_remote_copy(
            src_ref=source, dst_ref=target, send_sem=send.at[number], recv_sem=recv.at[number],
            device_id=where, device_id_type=MESH,
        )

    def start(source, target, number, where):
        one = copy(source, target, number, where)
        one.start()
        started.append(one)

    def arrived(target, number):
        copy(target, target, number, sibling).wait_recv()

    def lists_x(base):
        for offset in (1, 2, 3):
            block = lists.at[core, chip]
            start(block, block, base + offset - 1, device(turn(x, offset), z, core))

    def lists_z(base):
        for offset in (1, 2, 3):
            arrived(lists.at[core, z * RING + turn(x, 4 - offset)], base + offset - 1)
        row = lists.at[core, pl.ds(z * RING, RING)]
        for offset in (1, 2, 3):
            start(row, row, base + 2 + offset, device(x, turn(z, offset), core))

    def lists_across(base):
        for offset in (1, 2, 3):
            arrived(lists.at[core, pl.ds(turn(z, 4 - offset) * RING, RING)], base + 2 + offset)
        start(lists.at[core], lists.at[core], base + 6, sibling)

    def rows_x(buffer, base, outgoing):
        block = buffer.at[core, y, z]

        @pl.when(x == y)
        def _():
            for offset in (1, 2, 3):
                source = outgoing.at[turn(x, offset)] if outgoing is staged else block
                copy(source, block, base + offset - 1, device(turn(x, offset), z, core)).start()

    def rows_x_sent(buffer, base):
        @pl.when(x == y)
        def _():
            for offset in (1, 2, 3):
                copy(buffer.at[core, y, z], buffer.at[core, y, z], base + offset - 1, sibling).wait_send()

    def rows_z(buffer, base):
        block = buffer.at[core, y, z]

        @pl.when(x != y)
        def _():
            arrived(block, base + turn(x, 4 - y) - 1)

        for offset in (1, 2, 3):
            start(block, block, base + 2 + offset, device(x, turn(z, offset), core))

    def rows_y(buffer, base):
        for offset in (1, 2, 3):
            arrived(buffer.at[core, y, turn(z, 4 - offset)], base + 2 + offset)
        for offset in (1, 2, 3):
            block = buffer.at[core, y]
            start(block, block, base + 5 + offset, {"group": turn(y, offset)})

    def rows_across(buffer, base):
        for offset in (1, 2, 3):
            arrived(buffer.at[core, turn(y, 4 - offset)], base + 5 + offset)
        start(buffer.at[core], buffer.at[core], base + 9, sibling)

    def ended(buffer, number):
        arrived(buffer.at[1 - core], number)

    def piece(half, first, second, part=None):
        low, count = (96 * half, 96) if part is None else (96 * half + 48 * part, 48)
        where = slot(first, second) if half == 0 else slot(second, first)
        return img.at[where, pl.ds(low, count)]

    def neighbour(axis, direction):
        step = 1 if direction == 0 else 3
        return device(turn(x, step), z, core) if axis == 0 else device(x, turn(z, step), core)

    def first_ring(half, direction):
        start(piece(half, 0, 0), piece(half, 0, 0), 20 * half + direction, neighbour(half, direction))

    def first_forward(half, direction):
        block = piece(half, (3, 1)[direction], 0, direction)
        start(block, block, 20 * half + 2 + direction, neighbour(half, direction))

    def second_ring(half, k):
        for direction in (0, 1):
            block = piece(half, FIRST[k], 0)
            start(block, block, 20 * half + 4 + 4 * k + direction, neighbour(1 - half, direction))

    def second_forward(half, k, direction):
        block = piece(half, FIRST[k], (3, 1)[direction], direction)
        start(block, block, 20 * half + 6 + 4 * k + direction, neighbour(1 - half, direction))

    def got_first(half, direction):
        arrived(piece(half, (3, 1)[direction], 0), 20 * half + direction)

    def got_first_forward(half, direction):
        arrived(piece(half, 2, 0, direction), 20 * half + 2 + direction)

    def got_second(half, k, direction):
        arrived(piece(half, FIRST[k], (3, 1)[direction]), 20 * half + 4 + 4 * k + direction)

    def got_second_forward(half, k, direction):
        arrived(piece(half, FIRST[k], 2, direction), 20 * half + 6 + 4 * k + direction)

    def pair_copy(where, row):
        return pltpu.make_async_remote_copy(
            src_ref=kv.at[row], dst_ref=kv.at[row], send_sem=pair_send.at[where],
            recv_sem=pair_recv.at[where], device_id=sibling, device_id_type=MESH,
        )

    def project(count, offsets):
        def one(i, carried):
            where = slot(*offsets(i))
            row = where * 2 + core
            normed = img[where]
            kv[row, 0:WIDE, :] = lax.dot_general(
                normed, wt[WIDE:2 * WIDE, :], NT, preferred_element_type=F32
            ).astype(BF16)
            kv[row, WIDE:2 * WIDE, :] = lax.dot_general(
                wt[2 * WIDE:3 * WIDE, :], normed, NT, preferred_element_type=F32
            ).astype(BF16)
            pair_copy(where, row).start()
            return carried

        lax.fori_loop(0, count, one, 0)

    W0, L0, O0 = 40, 50, 57
    rows_x(wplane, W0, staged)
    lists_x(L0)
    for half in (0, 1):
        for direction in (0, 1):
            first_ring(half, direction)
        second_ring(half, 0)
    rows_z(wplane, W0)
    lists_z(L0)
    rows_x(woplane, O0, woplane)

    rows_y(wplane, W0)
    for direction in (0, 1):
        for half in (0, 1):
            got_first(half, direction)
            first_forward(half, direction)
            second_ring(half, 1 + direction)
    for direction in (0, 1):
        for half in (0, 1):
            got_second(half, 0, direction)
            second_forward(half, 0, direction)
    rows_across(wplane, W0)
    lists_across(L0)
    rows_z(woplane, O0)
    ended(wplane, W0 + 9)
    ended(lists, L0 + 6)

    for j in (0, 1):
        blocks = []
        for one in range(8 * j, 8 * j + 8):
            for c in (0, 1):
                blocks.append(wplane[c, one % RING, one // RING].astype(F32))
        wt[:, 384 * j:384 * (j + 1)] = jnp.concatenate(blocks, axis=0).T.astype(BF16)
    project(1, lambda i: (i, i))
    project(4, lambda i: ((1 + 2 * (i % 2)) * (1 - i // 2), (1 + 2 * (i % 2)) * (i // 2)))

    tables = [jnp.sum(lists[c], axis=0) for c in (0, 1)]
    attended = lax.broadcasted_iota(I32, (32, 128), 0)

    def weight_column(querying):
        taken = jnp.zeros((32, 128), I32)
        for table in tables:
            for here, there in ((0, 1), (1, 0)):
                given = jnp.where(table[here:here + 1, :] == querying, table[2 + here:3 + here, :], 0)
                taken = taken + jnp.where(table[there:there + 1, :] == attended, given, 0)
        return jnp.sum(taken, axis=1, keepdims=True)

    column = lax.broadcasted_iota(I32, (32, 128), 1)
    by_query = jnp.zeros((32, 128), I32)
    for i in range(RING):
        by_query = jnp.where(column == i, weight_column((z * RING + i) * 2 + core), by_query)
    weights[...] = by_query
    own = jnp.sum(weight_column(chip * 2 + core).astype(F32), axis=0, keepdims=True)
    total[...] = jnp.broadcast_to(1.0 + own, (8, 128))

    for half in (0, 1):
        for direction in (0, 1):
            got_first_forward(half, direction)
        second_ring(half, 3)
    for k in (1, 2):
        for direction in (0, 1):
            for half in (0, 1):
                got_second(half, k, direction)
                second_forward(half, k, direction)
    for half in (0, 1):
        for direction in (0, 1):
            got_second_forward(half, 0, direction)
    rows_y(woplane, O0)
    project(4, lambda i: (1 + 2 * (i // 2), 1 + 2 * (i % 2)))
    project(2, lambda i: (2 * (1 - i), 2 * i))

    def one_query(i, carried):
        query = lax.dot_general(
            wt[0:WIDE, :], img[z * RING + i], NT, preferred_element_type=F32
        ).astype(BF16)
        both[i] = jnp.zeros((128, 2 * SEQ), BF16)
        for h in (0, 1):
            both[i, 64 * h:64 * (h + 1), SEQ * h:SEQ * (h + 1)] = query[64 * h:64 * (h + 1), :]
        third[i] = query[128:192, :]
        return carried

    lax.fori_loop(0, RING, one_query, 0)

    for direction in (0, 1):
        for half in (0, 1):
            got_second(half, 3, direction)
            second_forward(half, 3, direction)
    for k in (1, 2):
        for direction in (0, 1):
            for half in (0, 1):
                got_second_forward(half, k, direction)
    rows_across(woplane, O0)
    project(4, lambda i: (
        2 * (1 - i // 2) + (1 + 2 * (i % 2)) * (i // 2),
        (1 + 2 * (i % 2)) * (1 - i // 2) + 2 * (i // 2),
    ))
    ended(woplane, O0 + 9)
    for one in range(PLANE):
        blocks = [woplane[c, one % RING, one // RING].astype(F32) for c in (0, 1)]
        wo_all[2 * ROWS * one:2 * ROWS * (one + 1), :] = jnp.concatenate(blocks, axis=0).astype(BF16)
    for half in (0, 1):
        for direction in (0, 1):
            got_second_forward(half, 3, direction)
    project(1, lambda i: (i + 2, i + 2))
    for one in started:
        one.wait_send()
    rows_x_sent(wplane, W0)
    rows_x_sent(woplane, O0)

    def drain(where, carried):
        pair_copy(where, where * 2 + core).wait_send()
        pair_copy(where, where * 2 + 1 - core).wait_recv()
        return carried

    lax.fori_loop(0, PLANE, drain, 0)


WINDOWS = ((0, 256, 0), (128, 384, 64), (0, 192, 0))
TOGETHER = 6


def attend_kernel(weights, kv, both, third, out, acc, chosen, chosen_weight):
    acc[...] = jnp.zeros_like(acc)

    def note(number, count):
        weight = weights[number // RING, number % RING]
        chosen[count] = number
        chosen_weight[count] = weight
        return count + jnp.where(weight > 0, 1, 0)

    count = lax.fori_loop(0, 128, note, 0, unroll=8)
    for extra in range(TOGETHER - 1):
        chosen[count + extra] = 0
        chosen_weight[count + extra] = 0
    factor = math.log2(math.e) / 8.0

    def attention(scores):
        top = jnp.max(scores, axis=0, keepdims=True)
        expo = jnp.exp2((scores - top) * factor)
        return expo.astype(BF16), 1.0 / jnp.sum(expo, axis=0, keepdims=True)

    def several(step, carried):
        entries = [TOGETHER * step + part for part in range(TOGETHER)]
        places = [(chosen[entry] // RING, chosen[entry] % RING) for entry in entries]
        given = [chosen_weight[entry].astype(F32) for entry in entries]
        scores = [
            (
                jnp.dot(kv[t, 0:WIDE, 0:128], both[i], preferred_element_type=F32),
                jnp.dot(kv[t, 0:WIDE, 128:192], third[i], preferred_element_type=F32),
            )
            for t, i in places
        ]
        shares = [[attention(part) for part in one] for one in scores]
        found = []
        for (t, _), share, weight in zip(places, shares, given):
            for h, (low, high, _) in enumerate(WINDOWS):
                expo, scale = share[h // 2]
                one = jnp.dot(
                    kv[t, WIDE + 64 * h:WIDE + 64 * (h + 1), :], expo[:, low:high],
                    preferred_element_type=F32,
                )
                found.append((one * scale[:, low:high]).astype(BF16).astype(F32) * weight)
        for n, (_, i) in enumerate(places):
            for h in range(3):
                one = found[3 * n + h]
                acc[i, h, :, 0:one.shape[1]] += one
        return carried

    lax.fori_loop(0, (count + TOGETHER - 1) // TOGETHER, several, 0)
    for i in range(RING):
        heads = [acc[i, h][:, low:low + SEQ] for h, (_, _, low) in enumerate(WINDOWS)]
        summed = jnp.concatenate(heads, axis=0).astype(BF16)
        out[i, 0:WIDE, :] = summed[:, 0:128]
        out[i, WIDE:WIDE + 96, :] = jnp.concatenate([summed[0:96, 128:192], summed[96:192, 128:192]], axis=1)


def output_kernel(attended, wo_all, total, out, held, summed, send, recv):
    x, z, core = place()
    barrier = pltpu.get_barrier_semaphore()
    for offset in (1, 2, 3):
        pl.semaphore_signal(
            barrier, 1, device_id=device(lax.rem(x + offset, RING), z, core), device_id_type=MESH
        )
    pl.semaphore_wait(barrier, 3)
    copies = []
    for offset in (1, 2, 3):
        peer = lax.rem(x + offset, RING)
        one = pltpu.make_async_remote_copy(
            src_ref=attended.at[peer], dst_ref=held.at[x], send_sem=send.at[offset - 1],
            recv_sem=recv.at[offset - 1], device_id=device(peer, z, core), device_id_type=MESH,
        )
        one.start()
        copies.append(one)

    def unpack(peer, block):
        row = pl.multiple_of(peer * WIDE, WIDE)
        summed[pl.ds(row, WIDE), 0:128] = block[0:WIDE, :]
        summed[pl.ds(row, 96), 128:192] = block[WIDE:WIDE + 96, 0:64]
        summed[pl.ds(row + 96, 96), 128:192] = block[WIDE:WIDE + 96, 64:128]

    unpack(x, attended[x])
    for offset in (1, 2, 3):
        peer = lax.rem(x + 4 - offset, RING)
        pltpu.make_async_remote_copy(
            src_ref=attended.at[peer], dst_ref=held.at[peer], send_sem=send.at[offset - 1],
            recv_sem=recv.at[offset - 1], device_id=device(peer, z, core), device_id_type=MESH,
        ).wait_recv()
        unpack(peer, held[peer])
    numerator = lax.dot_general(summed[...], wo_all[...], TN, preferred_element_type=F32)
    out[0] = (numerator / total[0:1, 0:1]).astype(BF16)
    for one in copies:
        one.wait_send()


VMEM = pl.BlockSpec(memory_space=pltpu.VMEM)
SMEM = pl.BlockSpec(memory_space=pltpu.SMEM)
HBM = pl.BlockSpec(memory_space=pltpu.HBM)


def shards(tokens, norm_gain, w_query, w_key, w_value, w_out, owner_map, pair_images, pair_count, confidence):
    kv, both, third, weights, total, wo_all = pl.pallas_call(
        gather_kernel,
        out_shape=(
            jax.ShapeDtypeStruct((2 * PLANE, 2 * WIDE, SEQ), BF16),
            jax.ShapeDtypeStruct((RING, 128, 2 * SEQ), BF16),
            jax.ShapeDtypeStruct((RING, 64, SEQ), BF16),
            jax.ShapeDtypeStruct((32, 128), I32),
            jax.ShapeDtypeStruct((8, 128), F32),
            jax.ShapeDtypeStruct((D, D), BF16),
        ),
        in_specs=[HBM] * 10,
        out_specs=(VMEM,) * 6,
        scratch_shapes=[
            pltpu.VMEM((1, SEQ, D), BF16),
            pltpu.VMEM((D,), F32),
            pltpu.VMEM((ROWS, D), BF16),
            pltpu.VMEM((ROWS, D), BF16),
            pltpu.VMEM((ROWS, D), BF16),
            pltpu.VMEM((ROWS, D), BF16),
            pltpu.VMEM((1, 32), I32),
            pltpu.VMEM((2, 8), I32),
            pltpu.SMEM((1,), I32),
            pltpu.VMEM((2, 8), I32),
            pltpu.VMEM((PLANE, SEQ, D), BF16),
            pltpu.VMEM((RING, ROWS, 640), BF16),
            pltpu.VMEM((2, RING, RING, ROWS, 640), BF16),
            pltpu.VMEM((2, RING, RING, ROWS, D), BF16),
            pltpu.VMEM((2, PLANE, 8, 128), I32),
            pltpu.VMEM((640, D), BF16),
            pltpu.SemaphoreType.DMA((10,)),
            pltpu.SemaphoreType.DMA((67,)),
            pltpu.SemaphoreType.DMA((67,)),
            pltpu.SemaphoreType.DMA((PLANE,)),
            pltpu.SemaphoreType.DMA((PLANE,)),
        ],
        compiler_params=pltpu.CompilerParams(
            collective_id=0, has_side_effects=True, vmem_limit_bytes=32 * 1024 * 1024
        ),
        name="gather_project",
    )(
        *[
            pltpu.with_memory_space_constraint(one, pltpu.HBM)
            for one in (tokens, norm_gain, w_query, w_key, w_value, w_out, owner_map, pair_images.T)
        ],
        pair_count, pltpu.with_memory_space_constraint(confidence.T, pltpu.HBM),
    )
    attended = pl.pallas_call(
        attend_kernel,
        out_shape=jax.ShapeDtypeStruct((RING, WIDE + 96, 128), BF16),
        in_specs=[SMEM, VMEM, VMEM, VMEM],
        out_specs=VMEM,
        scratch_shapes=[
            pltpu.VMEM((RING, 3, 64, 256), F32),
            pltpu.SMEM((136,), I32),
            pltpu.SMEM((136,), I32),
        ],
        compiler_params=pltpu.CompilerParams(vmem_limit_bytes=32 * 1024 * 1024),
        name="attend",
    )(weights, kv, both, third)
    return pl.pallas_call(
        output_kernel,
        out_shape=jax.ShapeDtypeStruct((1, SEQ, D), BF16),
        in_specs=[VMEM] * 3,
        out_specs=VMEM,
        scratch_shapes=[
            pltpu.VMEM((RING, WIDE + 96, 128), BF16),
            pltpu.VMEM((D, SEQ), BF16),
            pltpu.SemaphoreType.DMA((3,)),
            pltpu.SemaphoreType.DMA((3,)),
        ],
        compiler_params=pltpu.CompilerParams(
            collective_id=1, has_side_effects=True, vmem_limit_bytes=32 * 1024 * 1024
        ),
        name="exchange_output",
    )(attended, wo_all, total)


def solution(mesh):
    both = P(("group", "shard"))
    in_specs = (
        P(("group", "shard"), None, None),
        P(),
        P("shard", None),
        P("shard", None),
        P("shard", None),
        P("shard", None),
        P("group", None),
        P(("group", "shard"), None),
        both,
        P(("group", "shard"), None),
    )
    out_specs = P(("group", "shard"), None, None)
    return jax.shard_map(shards, mesh=mesh, in_specs=in_specs, out_specs=out_specs, check_vma=False)
```

```python
import math

import jax
import jax.numpy as jnp
from jax import lax
from jax.experimental import pallas as pl
from jax.experimental.pallas import tpu as pltpu
from jax.sharding import PartitionSpec as P

MESH = pl.DeviceIdType.MESH
F32, BF16, I32 = jnp.float32, jnp.bfloat16, jnp.int32
SEQ, D, RING, PLANE = 192, 768, 4, 16
WIDE = 192
ROWS = 24
NT = (((1,), (1,)), ((), ()))
TN = (((0,), (0,)), ((), ()))
FIRST = (0, 3, 1, 2)


def place():
    shard = lax.axis_index("shard")
    core = lax.rem(shard, 2)
    chip = lax.div(shard, 2)
    return lax.rem(chip, RING), lax.div(chip, RING), core


def device(x, z, core):
    return {"shard": (z * RING + x) * 2 + core}


def gather_kernel(
    tok_h, gain_h, wq_h, wk_h, wv_h, wo_h, omap_h, pimg_h, pcnt_h, conf_h,
    kv, both, third, weights, total, wo_all,
    tok, gain, wq, wk, wv, wo, omap, pimg, pcnt, conf,
    img, passed, taken, staged, wplane, woplane, lists, wt, load, send, recv, pair_send, pair_recv,
):
    x, z, core = place()
    y = lax.axis_index("group")
    chip = z * RING + x

    def turn(value, offset):
        return lax.rem(value + offset, RING)

    def slot(ox, oz):
        return turn(z, oz) * RING + turn(x, ox)

    sibling = device(x, z, 1 - core)
    loads = [
        pltpu.make_async_copy(source, target, load.at[n])
        for n, (source, target) in enumerate((
            (tok_h, tok), (gain_h, gain), (wq_h, wq), (wk_h, wk), (wv_h, wv), (wo_h, wo),
            (omap_h, omap), (pimg_h, pimg), (pcnt_h, pcnt), (conf_h, conf),
        ))
    ]
    for one in loads:
        one.start()
    barrier = pltpu.get_barrier_semaphore()
    for offset in (1, 2, 3):
        for peer in (device(turn(x, offset), z, core), device(x, turn(z, offset), core), {"group": turn(y, offset)}):
            pl.semaphore_signal(barrier, 1, device_id=peer, device_id_type=MESH)
    pl.semaphore_signal(barrier, 1, device_id=sibling, device_id_type=MESH)

    for one in loads:
        one.wait()
    values = tok[0].astype(F32)
    centred = values - jnp.mean(values, axis=-1, keepdims=True)
    variance = jnp.mean(centred * centred, axis=-1, keepdims=True)
    img[chip] = (centred * lax.rsqrt(variance + 1e-05) * gain[...].reshape(1, D)).astype(BF16)

    square = (lax.broadcasted_iota(I32, (32, 32), 0), lax.broadcasted_iota(I32, (32, 32), 1))
    owners = jnp.sum(jnp.where(square[0] == square[1], omap[...], 0), axis=1, keepdims=True)
    image = lax.broadcasted_iota(I32, (32, 8), 0)
    stored = [
        jnp.sum(jnp.where(pimg[r:r + 1, :] == image, owners, 0), axis=0, keepdims=True) for r in (0, 1)
    ]
    listed = lax.broadcasted_iota(I32, (2, 8), 1) < pcnt[0]
    entries = jnp.concatenate(stored + [jnp.where(listed, conf[...], 0), jnp.zeros((4, 8), I32)], axis=0)
    entries = jnp.concatenate([entries, jnp.zeros((8, 120), I32)], axis=1)
    lists[core, chip] = pltpu.roll(entries, 8 * chip, 1)

    @pl.when(x == y)
    def _():
        parts = [w[...].astype(F32) for w in (wq, wk, wv)]
        for g in range(RING):
            cols = [w[:, g * WIDE:(g + 1) * WIDE] for w in parts] + [jnp.zeros((ROWS, 64), F32)]
            staged[g] = jnp.concatenate(cols, axis=1).astype(BF16)
        wplane[core, y, z] = staged[x]
        woplane[core, y, z] = wo[...]

    pl.semaphore_wait(barrier, 10)

    started = []

    def copy(source, target, number, where):
        return pltpu.make_async_remote_copy(
            src_ref=source, dst_ref=target, send_sem=send.at[number], recv_sem=recv.at[number],
            device_id=where, device_id_type=MESH,
        )

    def start(source, target, number, where):
        one = copy(source, target, number, where)
        one.start()
        started.append(one)

    def arrived(target, number):
        copy(target, target, number, sibling).wait_recv()

    def lists_x(base):
        for offset in (1, 2, 3):
            block = lists.at[core, chip]
            start(block, block, base + offset - 1, device(turn(x, offset), z, core))

    def lists_z(base):
        for offset in (1, 2, 3):
            arrived(lists.at[core, z * RING + turn(x, 4 - offset)], base + offset - 1)
        row = lists.at[core, pl.ds(z * RING, RING)]
        for offset in (1, 2, 3):
            start(row, row, base + 2 + offset, device(x, turn(z, offset), core))

    def lists_across(base):
        for offset in (1, 2, 3):
            arrived(lists.at[core, pl.ds(turn(z, 4 - offset) * RING, RING)], base + 2 + offset)
        start(lists.at[core], lists.at[core], base + 6, sibling)

    def rows_x(buffer, base, outgoing):
        block = buffer.at[core, y, z]

        @pl.when(x == y)
        def _():
            for offset in (1, 2, 3):
                source = outgoing.at[turn(x, offset)] if outgoing is staged else block
                copy(source, block, base + offset - 1, device(turn(x, offset), z, core)).start()

    def rows_x_sent(buffer, base):
        @pl.when(x == y)
        def _():
            for offset in (1, 2, 3):
                copy(buffer.at[core, y, z], buffer.at[core, y, z], base + offset - 1, sibling).wait_send()

    def rows_z(buffer, base):
        block = buffer.at[core, y, z]

        @pl.when(x != y)
        def _():
            arrived(block, base + turn(x, 4 - y) - 1)

        for offset in (1, 2, 3):
            start(block, block, base + 2 + offset, device(x, turn(z, offset), core))

    def rows_y(buffer, base):
        for offset in (1, 2, 3):
            arrived(buffer.at[core, y, turn(z, 4 - offset)], base + 2 + offset)
        for offset in (1, 2, 3):
            block = buffer.at[core, y]
            start(block, block, base + 5 + offset, {"group": turn(y, offset)})

    def rows_across(buffer, base):
        for offset in (1, 2, 3):
            arrived(buffer.at[core, turn(y, 4 - offset)], base + 5 + offset)
        start(buffer.at[core], buffer.at[core], base + 9, sibling)

    def ended(buffer, number):
        arrived(buffer.at[1 - core], number)

    def piece(ring, offset, half, part=None):
        low, count = (96 * half, 96) if part is None else (96 * half + 48 * part, 48)
        where = (slot(offset, 0), slot(0, offset), slot(offset, 2))[ring]
        return img.at[where, pl.ds(low, count)]

    def ring_send(ring, offset, half, part, direction, number):
        step = (1, 3)[direction]
        peer = device(x, turn(z, step), core) if ring == 1 else device(turn(x, step), z, core)
        block = piece(ring, offset, half, part)
        start(block, block, 8 * ring + 4 * half + number + direction, peer)

    def ring_start(ring, half):
        for direction in (0, 1):
            ring_send(ring, 0, half, None, direction, 0)

    def ring_pass(ring, half):
        for direction in (0, 1):
            arrived(piece(ring, (3, 1)[direction], half), 8 * ring + 4 * half + direction)
            ring_send(ring, (3, 1)[direction], half, direction, direction, 2)

    def ring_end(ring, half):
        for direction in (0, 1):
            arrived(piece(ring, 2, half, direction), 8 * ring + 4 * half + 2 + direction)

    def pair_copy(where, row):
        return pltpu.make_async_remote_copy(
            src_ref=kv.at[row], dst_ref=kv.at[row], send_sem=pair_send.at[where],
            recv_sem=pair_recv.at[where], device_id=sibling, device_id_type=MESH,
        )

    def projected(where):
        normed = img[where]
        keys = lax.dot_general(normed, wt[WIDE:2 * WIDE, :], NT, preferred_element_type=F32)
        values = lax.dot_general(wt[2 * WIDE:3 * WIDE, :], normed, NT, preferred_element_type=F32)
        kv[where * 2 + core, 0:WIDE, :] = keys.astype(BF16)
        kv[where * 2 + core, WIDE:2 * WIDE, :] = values.astype(BF16)
        pair_copy(where, where * 2 + core).start()
        return keys, values

    def project(count, offsets):
        def one(i, carried):
            projected(slot(*offsets(i)))
            return carried

        lax.fori_loop(0, count, one, 0)

    def project_and_pass(k):
        keys, values = projected(slot(FIRST[k], 0))
        passed[k - 1, 0:WIDE, :] = keys[:, 0:128].astype(BF16)
        passed[k - 1, WIDE:2 * WIDE, :] = values[:, 0:128].astype(BF16)
        passed[k - 1, 2 * WIDE:3 * WIDE, :] = jnp.concatenate(
            [keys[:, 128:WIDE], values[:, 128:WIDE]], axis=1
        ).astype(BF16)
        for direction in (0, 1):
            start(
                passed.at[k - 1], taken.at[direction, k - 1], 22 + 2 * k + direction,
                device(x, turn(z, (1, 3)[direction]), core),
            )

    def take(k):
        for direction in (0, 1):
            block = taken.at[direction, k - 1]
            arrived(block, 22 + 2 * k + direction)
            where = slot(FIRST[k], (3, 1)[direction])
            row = where * 2 + core
            kv[row, :, 0:128] = block[0:2 * WIDE, :]
            rest = block[2 * WIDE:3 * WIDE, :].astype(F32)
            kv[row, 0:WIDE, 128:WIDE] = rest[:, 0:64].astype(BF16)
            kv[row, WIDE:2 * WIDE, 128:WIDE] = rest[:, 64:128].astype(BF16)
            pair_copy(where, row).start()

    W0, L0, O0 = 30, 40, 47
    rows_x(wplane, W0, staged)
    lists_x(L0)
    ring_start(0, 0)
    ring_start(1, 0)
    ring_start(0, 1)
    rows_z(wplane, W0)
    ring_start(1, 1)
    rows_x(woplane, O0, woplane)
    lists_z(L0)
    ring_pass(0, 0)
    ring_pass(1, 0)
    rows_y(wplane, W0)
    ring_pass(1, 1)
    ring_pass(0, 1)
    rows_z(woplane, O0)
    ring_end(1, 0)
    ring_start(2, 0)
    rows_across(wplane, W0)
    ring_end(1, 1)
    ring_start(2, 1)
    lists_across(L0)
    ended(wplane, W0 + 9)

    for j in (0, 1):
        blocks = []
        for one in range(8 * j, 8 * j + 8):
            for c in (0, 1):
                blocks.append(wplane[c, one % RING, one // RING].astype(F32))
        wt[:, 384 * j:384 * (j + 1)] = jnp.concatenate(blocks, axis=0).T.astype(BF16)
    project_and_pass(1)
    project_and_pass(2)
    ring_end(0, 0)
    ring_end(0, 1)
    project_and_pass(3)
    rows_y(woplane, O0)
    project(4, lambda i: (0, i))
    ended(lists, L0 + 6)

    def one_query(i, carried):
        query = lax.dot_general(
            wt[0:WIDE, :], img[z * RING + i], NT, preferred_element_type=F32
        ).astype(BF16)
        both[i] = jnp.zeros((128, 2 * SEQ), BF16)
        for h in (0, 1):
            both[i, 64 * h:64 * (h + 1), SEQ * h:SEQ * (h + 1)] = query[64 * h:64 * (h + 1), :]
        third[i] = query[128:192, :]
        return carried

    lax.fori_loop(0, RING, one_query, 0)

    tables = [jnp.sum(lists[c], axis=0) for c in (0, 1)]
    attended = lax.broadcasted_iota(I32, (32, 128), 0)

    def weight_column(querying):
        taken = jnp.zeros((32, 128), I32)
        for table in tables:
            for here, there in ((0, 1), (1, 0)):
                given = jnp.where(table[here:here + 1, :] == querying, table[2 + here:3 + here, :], 0)
                taken = taken + jnp.where(table[there:there + 1, :] == attended, given, 0)
        return jnp.sum(taken, axis=1, keepdims=True)

    column = lax.broadcasted_iota(I32, (32, 128), 1)
    by_query = jnp.zeros((32, 128), I32)
    for i in range(RING):
        by_query = jnp.where(column == i, weight_column((z * RING + i) * 2 + core), by_query)
    weights[...] = by_query
    own = jnp.sum(weight_column(chip * 2 + core).astype(F32), axis=0, keepdims=True)
    total[...] = jnp.broadcast_to(1.0 + own, (8, 128))

    ring_pass(2, 0)
    take(1)
    ring_pass(2, 1)
    project(2, lambda i: (1 + 2 * i, 2))
    rows_across(woplane, O0)
    take(2)
    ring_end(2, 0)
    ring_end(2, 1)
    project(1, lambda i: (i + 2, i + 2))
    ended(woplane, O0 + 9)
    for one in range(PLANE):
        blocks = [woplane[c, one % RING, one // RING].astype(F32) for c in (0, 1)]
        wo_all[2 * ROWS * one:2 * ROWS * (one + 1), :] = jnp.concatenate(blocks, axis=0).astype(BF16)
    take(3)

    for one in started:
        one.wait_send()
    rows_x_sent(wplane, W0)
    rows_x_sent(woplane, O0)

    def drain(where, carried):
        pair_copy(where, where * 2 + core).wait_send()
        pair_copy(where, where * 2 + 1 - core).wait_recv()
        return carried

    lax.fori_loop(0, PLANE, drain, 0)


WINDOWS = ((0, 256, 0), (128, 384, 64), (0, 192, 0))
TOGETHER = 6


def attend_kernel(weights, kv, both, third, out, acc, chosen, chosen_weight):
    acc[...] = jnp.zeros_like(acc)

    def note(number, count):
        weight = weights[number // RING, number % RING]
        chosen[count] = number
        chosen_weight[count] = weight
        return count + jnp.where(weight > 0, 1, 0)

    count = lax.fori_loop(0, 128, note, 0, unroll=8)
    for extra in range(TOGETHER - 1):
        chosen[count + extra] = 0
        chosen_weight[count + extra] = 0
    factor = math.log2(math.e) / 8.0

    def attention(scores):
        top = jnp.max(scores, axis=0, keepdims=True)
        expo = jnp.exp2((scores - top) * factor)
        return expo.astype(BF16), 1.0 / jnp.sum(expo, axis=0, keepdims=True)

    def several(step, carried):
        entries = [TOGETHER * step + part for part in range(TOGETHER)]
        places = [(chosen[entry] // RING, chosen[entry] % RING) for entry in entries]
        given = [chosen_weight[entry].astype(F32) for entry in entries]
        scores = [
            (
                jnp.dot(kv[t, 0:WIDE, 0:128], both[i], preferred_element_type=F32),
                jnp.dot(kv[t, 0:WIDE, 128:192], third[i], preferred_element_type=F32),
            )
            for t, i in places
        ]
        shares = [[attention(part) for part in one] for one in scores]
        found = []
        for (t, _), share, weight in zip(places, shares, given):
            for h, (low, high, _) in enumerate(WINDOWS):
                expo, scale = share[h // 2]
                one = jnp.dot(
                    kv[t, WIDE + 64 * h:WIDE + 64 * (h + 1), :], expo[:, low:high],
                    preferred_element_type=F32,
                )
                found.append((one * scale[:, low:high]).astype(BF16).astype(F32) * weight)
        for n, (_, i) in enumerate(places):
            for h in range(3):
                one = found[3 * n + h]
                acc[i, h, :, 0:one.shape[1]] += one
        return carried

    lax.fori_loop(0, (count + TOGETHER - 1) // TOGETHER, several, 0)
    for i in range(RING):
        heads = [acc[i, h][:, low:low + SEQ] for h, (_, _, low) in enumerate(WINDOWS)]
        summed = jnp.concatenate(heads, axis=0).astype(BF16)
        out[i, 0:WIDE, :] = summed[:, 0:128]
        out[i, WIDE:WIDE + 96, :] = jnp.concatenate([summed[0:96, 128:192], summed[96:192, 128:192]], axis=1)


def output_kernel(attended, wo_all, total, out, held, summed, send, recv):
    x, z, core = place()
    barrier = pltpu.get_barrier_semaphore()
    for offset in (1, 2, 3):
        pl.semaphore_signal(
            barrier, 1, device_id=device(lax.rem(x + offset, RING), z, core), device_id_type=MESH
        )
    pl.semaphore_wait(barrier, 3)
    copies = []
    for offset in (1, 2, 3):
        peer = lax.rem(x + offset, RING)
        one = pltpu.make_async_remote_copy(
            src_ref=attended.at[peer], dst_ref=held.at[x], send_sem=send.at[offset - 1],
            recv_sem=recv.at[offset - 1], device_id=device(peer, z, core), device_id_type=MESH,
        )
        one.start()
        copies.append(one)

    def unpack(peer, block):
        row = pl.multiple_of(peer * WIDE, WIDE)
        summed[pl.ds(row, WIDE), 0:128] = block[0:WIDE, :]
        summed[pl.ds(row, 96), 128:192] = block[WIDE:WIDE + 96, 0:64]
        summed[pl.ds(row + 96, 96), 128:192] = block[WIDE:WIDE + 96, 64:128]

    unpack(x, attended[x])
    for offset in (1, 2, 3):
        peer = lax.rem(x + 4 - offset, RING)
        pltpu.make_async_remote_copy(
            src_ref=attended.at[peer], dst_ref=held.at[peer], send_sem=send.at[offset - 1],
            recv_sem=recv.at[offset - 1], device_id=device(peer, z, core), device_id_type=MESH,
        ).wait_recv()
        unpack(peer, held[peer])
    numerator = lax.dot_general(summed[...], wo_all[...], TN, preferred_element_type=F32)
    out[0] = (numerator / total[0:1, 0:1]).astype(BF16)
    for one in copies:
        one.wait_send()


VMEM = pl.BlockSpec(memory_space=pltpu.VMEM)
SMEM = pl.BlockSpec(memory_space=pltpu.SMEM)
HBM = pl.BlockSpec(memory_space=pltpu.HBM)


def shards(tokens, norm_gain, w_query, w_key, w_value, w_out, owner_map, pair_images, pair_count, confidence):
    kv, both, third, weights, total, wo_all = pl.pallas_call(
        gather_kernel,
        out_shape=(
            jax.ShapeDtypeStruct((2 * PLANE, 2 * WIDE, SEQ), BF16),
            jax.ShapeDtypeStruct((RING, 128, 2 * SEQ), BF16),
            jax.ShapeDtypeStruct((RING, 64, SEQ), BF16),
            jax.ShapeDtypeStruct((32, 128), I32),
            jax.ShapeDtypeStruct((8, 128), F32),
            jax.ShapeDtypeStruct((D, D), BF16),
        ),
        in_specs=[HBM] * 10,
        out_specs=(VMEM,) * 6,
        scratch_shapes=[
            pltpu.VMEM((1, SEQ, D), BF16),
            pltpu.VMEM((D,), F32),
            pltpu.VMEM((ROWS, D), BF16),
            pltpu.VMEM((ROWS, D), BF16),
            pltpu.VMEM((ROWS, D), BF16),
            pltpu.VMEM((ROWS, D), BF16),
            pltpu.VMEM((1, 32), I32),
            pltpu.VMEM((2, 8), I32),
            pltpu.SMEM((1,), I32),
            pltpu.VMEM((2, 8), I32),
            pltpu.VMEM((PLANE, SEQ, D), BF16),
            pltpu.VMEM((3, 3 * WIDE, 128), BF16),
            pltpu.VMEM((2, 3, 3 * WIDE, 128), BF16),
            pltpu.VMEM((RING, ROWS, 640), BF16),
            pltpu.VMEM((2, RING, RING, ROWS, 640), BF16),
            pltpu.VMEM((2, RING, RING, ROWS, D), BF16),
            pltpu.VMEM((2, PLANE, 8, 128), I32),
            pltpu.VMEM((640, D), BF16),
            pltpu.SemaphoreType.DMA((10,)),
            pltpu.SemaphoreType.DMA((57,)),
            pltpu.SemaphoreType.DMA((57,)),
            pltpu.SemaphoreType.DMA((PLANE,)),
            pltpu.SemaphoreType.DMA((PLANE,)),
        ],
        compiler_params=pltpu.CompilerParams(
            collective_id=0, has_side_effects=True, vmem_limit_bytes=32 * 1024 * 1024
        ),
        name="gather_project",
    )(
        *[
            pltpu.with_memory_space_constraint(one, pltpu.HBM)
            for one in (tokens, norm_gain, w_query, w_key, w_value, w_out, owner_map, pair_images.T)
        ],
        pair_count, pltpu.with_memory_space_constraint(confidence.T, pltpu.HBM),
    )
    attended = pl.pallas_call(
        attend_kernel,
        out_shape=jax.ShapeDtypeStruct((RING, WIDE + 96, 128), BF16),
        in_specs=[SMEM, VMEM, VMEM, VMEM],
        out_specs=VMEM,
        scratch_shapes=[
            pltpu.VMEM((RING, 3, 64, 256), F32),
            pltpu.SMEM((136,), I32),
            pltpu.SMEM((136,), I32),
        ],
        compiler_params=pltpu.CompilerParams(vmem_limit_bytes=32 * 1024 * 1024),
        name="attend",
    )(weights, kv, both, third)
    return pl.pallas_call(
        output_kernel,
        out_shape=jax.ShapeDtypeStruct((1, SEQ, D), BF16),
        in_specs=[VMEM] * 3,
        out_specs=VMEM,
        scratch_shapes=[
            pltpu.VMEM((RING, WIDE + 96, 128), BF16),
            pltpu.VMEM((D, SEQ), BF16),
            pltpu.SemaphoreType.DMA((3,)),
            pltpu.SemaphoreType.DMA((3,)),
        ],
        compiler_params=pltpu.CompilerParams(
            collective_id=1, has_side_effects=True, vmem_limit_bytes=32 * 1024 * 1024
        ),
        name="exchange_output",
    )(attended, wo_all, total)


def solution(mesh):
    both = P(("group", "shard"))
    in_specs = (
        P(("group", "shard"), None, None),
        P(),
        P("shard", None),
        P("shard", None),
        P("shard", None),
        P("shard", None),
        P("group", None),
        P(("group", "shard"), None),
        both,
        P(("group", "shard"), None),
    )
    out_specs = P(("group", "shard"), None, None)
    return jax.shard_map(shards, mesh=mesh, in_specs=in_specs, out_specs=out_specs, check_vma=False)
```

```python
import math

import jax
import jax.numpy as jnp
from jax import lax
from jax.experimental import pallas as pl
from jax.experimental.pallas import tpu as pltpu
from jax.sharding import PartitionSpec as P

MESH = pl.DeviceIdType.MESH
F32, BF16, I32 = jnp.float32, jnp.bfloat16, jnp.int32
SEQ, D, RING, PLANE = 192, 768, 4, 16
WIDE = 192
ROWS = 24
NT = (((1,), (1,)), ((), ()))
TN = (((0,), (0,)), ((), ()))
FIRST = (0, 3, 1, 2)


def place():
    shard = lax.axis_index("shard")
    core = lax.rem(shard, 2)
    chip = lax.div(shard, 2)
    return lax.rem(chip, RING), lax.div(chip, RING), core


def device(x, z, core):
    return {"shard": (z * RING + x) * 2 + core}


def in_order(planes, j):
    blocks = [
        planes[c][one % RING, one // RING].astype(F32) for one in range(8 * j, 8 * j + 8) for c in (0, 1)
    ]
    return jnp.concatenate(blocks, axis=0)


def gather_kernel(
    tok_h, gain_h, wq_h, wk_h, wv_h, wo_h, omap_h, pimg_h, pcnt, conf_h,
    kv, both, third, directions, total, woplane,
    tok, gain, wq, wk, wv, wo, omap, pimg, conf,
    img, passed, taken, staged, staged_query, wplane, qplane, lists, wt, load, send, recv, pair_send, pair_recv,
):
    x, z, core = place()
    y = lax.axis_index("group")
    chip = z * RING + x

    def turn(value, offset):
        return lax.rem(value + offset, RING)

    def slot(ox, oz):
        return turn(z, oz) * RING + turn(x, ox)

    sibling = device(x, z, 1 - core)
    loads = [
        pltpu.make_async_copy(source, target, load.at[n])
        for n, (source, target) in enumerate((
            (tok_h, tok), (gain_h, gain), (wq_h, wq), (wk_h, wk), (wv_h, wv), (wo_h, wo),
            (omap_h, omap), (pimg_h, pimg), (conf_h, conf),
        ))
    ]
    for one in loads:
        one.start()
    barrier = pltpu.get_barrier_semaphore()
    for offset in (1, 2, 3):
        for peer in (device(turn(x, offset), z, core), device(x, turn(z, offset), core), {"group": turn(y, offset)}):
            pl.semaphore_signal(barrier, 1, device_id=peer, device_id_type=MESH)
    pl.semaphore_signal(barrier, 1, device_id=sibling, device_id_type=MESH)

    for one in loads:
        one.wait()
    values = tok[0].astype(F32)
    centred = values - jnp.mean(values, axis=-1, keepdims=True)
    variance = jnp.mean(centred * centred, axis=-1, keepdims=True)
    img[chip] = (centred * lax.rsqrt(variance + 1e-05) * gain[...].reshape(1, D)).astype(BF16)

    square = (lax.broadcasted_iota(I32, (32, 32), 0), lax.broadcasted_iota(I32, (32, 32), 1))
    owners = jnp.sum(jnp.where(square[0] == square[1], omap[...], 0), axis=1, keepdims=True)
    image = lax.broadcasted_iota(I32, (32, 8), 0)
    stored = [
        jnp.sum(jnp.where(pimg[r:r + 1, :] == image, owners, 0), axis=0, keepdims=True) for r in (0, 1)
    ]
    listed = lax.broadcasted_iota(I32, (2, 8), 1) < pcnt[...]
    entries = jnp.concatenate(stored + [jnp.where(listed, conf[...], 0), jnp.zeros((4, 8), I32)], axis=0)
    entries = jnp.concatenate([entries, jnp.zeros((8, 120), I32)], axis=1)
    lists[core, chip] = pltpu.roll(entries, 8 * chip, 1)

    @pl.when(x == y)
    def _():
        keys, values, queries = [w[...].astype(F32) for w in (wk, wv, wq)]
        for g in range(RING):
            low, high = g * WIDE, (g + 1) * WIDE
            staged[g] = jnp.concatenate([keys[:, low:high], values[:, low:high]], axis=1).astype(BF16)
            staged_query[g] = jnp.concatenate(
                [queries[:, low:high], jnp.zeros((ROWS, 64), F32)], axis=1
            ).astype(BF16)
        wplane[core, y, z] = staged[x]
        qplane[core, y, z] = staged_query[x]
        woplane[core, y, z] = wo[...]

    pl.semaphore_wait(barrier, 10)

    started = []

    def copy(source, target, number, where):
        return pltpu.make_async_remote_copy(
            src_ref=source, dst_ref=target, send_sem=send.at[number], recv_sem=recv.at[number],
            device_id=where, device_id_type=MESH,
        )

    def start(source, target, number, where):
        one = copy(source, target, number, where)
        one.start()
        started.append(one)

    def arrived(target, number):
        copy(target, target, number, sibling).wait_recv()

    def lists_x(base):
        for offset in (1, 2, 3):
            block = lists.at[core, chip]
            start(block, block, base + offset - 1, device(turn(x, offset), z, core))

    def lists_z(base):
        for offset in (1, 2, 3):
            arrived(lists.at[core, z * RING + turn(x, 4 - offset)], base + offset - 1)
        row = lists.at[core, pl.ds(z * RING, RING)]
        for offset in (1, 2, 3):
            start(row, row, base + 2 + offset, device(x, turn(z, offset), core))

    def lists_across(base):
        for offset in (1, 2, 3):
            arrived(lists.at[core, pl.ds(turn(z, 4 - offset) * RING, RING)], base + 2 + offset)
        start(lists.at[core], lists.at[core], base + 6, sibling)

    def rows_x(buffer, base, outgoing):
        block = buffer.at[core, y, z]

        @pl.when(x == y)
        def _():
            for offset in (1, 2, 3):
                source = block if outgoing is None else outgoing.at[turn(x, offset)]
                copy(source, block, base + offset - 1, device(turn(x, offset), z, core)).start()

    def rows_x_sent(buffer, base):
        @pl.when(x == y)
        def _():
            for offset in (1, 2, 3):
                copy(buffer.at[core, y, z], buffer.at[core, y, z], base + offset - 1, sibling).wait_send()

    def rows_z(buffer, base):
        block = buffer.at[core, y, z]

        @pl.when(x != y)
        def _():
            arrived(block, base + turn(x, 4 - y) - 1)

        for offset in (1, 2, 3):
            start(block, block, base + 2 + offset, device(x, turn(z, offset), core))

    def rows_y(buffer, base):
        for offset in (1, 2, 3):
            arrived(buffer.at[core, y, turn(z, 4 - offset)], base + 2 + offset)
        for offset in (1, 2, 3):
            block = buffer.at[core, y]
            start(block, block, base + 5 + offset, {"group": turn(y, offset)})

    def rows_across(buffer, base):
        for offset in (1, 2, 3):
            arrived(buffer.at[core, turn(y, 4 - offset)], base + 5 + offset)
        start(buffer.at[core], buffer.at[core], base + 9, sibling)

    def ended(buffer, number):
        arrived(buffer.at[1 - core], number)

    def piece(ring, offset, half, part=None):
        low, count = (96 * half, 96) if part is None else (96 * half + 48 * part, 48)
        where = (slot(offset, 0), slot(0, offset), slot(offset, 2))[ring]
        return img.at[where, pl.ds(low, count)]

    def ring_send(ring, offset, half, part, direction, number):
        step = (1, 3)[direction]
        peer = device(x, turn(z, step), core) if ring == 1 else device(turn(x, step), z, core)
        block = piece(ring, offset, half, part)
        start(block, block, 8 * ring + 4 * half + number + direction, peer)

    def ring_start(ring, half):
        for direction in (0, 1):
            ring_send(ring, 0, half, None, direction, 0)

    def ring_pass(ring, half):
        for direction in (0, 1):
            arrived(piece(ring, (3, 1)[direction], half), 8 * ring + 4 * half + direction)
            ring_send(ring, (3, 1)[direction], half, direction, direction, 2)

    def ring_end(ring, half):
        for direction in (0, 1):
            arrived(piece(ring, 2, half, direction), 8 * ring + 4 * half + 2 + direction)

    def pair_copy(where, row):
        return pltpu.make_async_remote_copy(
            src_ref=kv.at[row], dst_ref=kv.at[row], send_sem=pair_send.at[where],
            recv_sem=pair_recv.at[where], device_id=sibling, device_id_type=MESH,
        )

    def projected(where):
        normed = img[where]
        keys = lax.dot_general(normed, wt[0:WIDE, :], NT, preferred_element_type=F32)
        values = lax.dot_general(wt[WIDE:2 * WIDE, :], normed, NT, preferred_element_type=F32)
        kv[where * 2 + core, 0:WIDE, :] = keys.astype(BF16)
        kv[where * 2 + core, WIDE:2 * WIDE, :] = values.astype(BF16)
        pair_copy(where, where * 2 + core).start()
        return keys, values

    def project(count, offsets):
        def one(i, carried):
            projected(slot(*offsets(i)))
            return carried

        lax.fori_loop(0, count, one, 0)

    def project_and_pass(k):
        keys, values = projected(slot(FIRST[k], 0))
        passed[k - 1, 0:WIDE, :] = keys[:, 0:128].astype(BF16)
        passed[k - 1, WIDE:2 * WIDE, :] = values[:, 0:128].astype(BF16)
        passed[k - 1, 2 * WIDE:3 * WIDE, :] = jnp.concatenate(
            [keys[:, 128:WIDE], values[:, 128:WIDE]], axis=1
        ).astype(BF16)
        for direction in (0, 1):
            start(
                passed.at[k - 1], taken.at[direction, k - 1], 22 + 2 * k + direction,
                device(x, turn(z, (1, 3)[direction]), core),
            )

    def take(k):
        for direction in (0, 1):
            block = taken.at[direction, k - 1]
            arrived(block, 22 + 2 * k + direction)
            where = slot(FIRST[k], (3, 1)[direction])
            row = where * 2 + core
            kv[row, :, 0:128] = block[0:2 * WIDE, :]
            rest = block[2 * WIDE:3 * WIDE, :].astype(F32)
            kv[row, 0:WIDE, 128:WIDE] = rest[:, 0:64].astype(BF16)
            kv[row, WIDE:2 * WIDE, 128:WIDE] = rest[:, 64:128].astype(BF16)
            pair_copy(where, row).start()

    W0, L0, O0, Q0 = 30, 40, 47, 57
    rows_x(wplane, W0, staged)
    rows_x(qplane, Q0, staged_query)
    lists_x(L0)
    ring_start(0, 0)
    ring_start(1, 0)
    ring_start(0, 1)
    rows_x(woplane, O0, None)
    rows_z(wplane, W0)
    rows_z(qplane, Q0)
    ring_start(1, 1)
    lists_z(L0)
    ring_pass(0, 0)
    ring_pass(1, 0)
    rows_y(wplane, W0)
    ring_pass(1, 1)
    rows_z(woplane, O0)
    ring_pass(0, 1)
    rows_y(qplane, Q0)
    ring_end(1, 0)
    ring_start(2, 0)
    rows_across(wplane, W0)
    ring_end(1, 1)
    ring_start(2, 1)
    lists_across(L0)
    ended(wplane, W0 + 9)

    for j in (0, 1):
        wt[0:2 * WIDE, 384 * j:384 * (j + 1)] = in_order([wplane.at[0], wplane.at[1]], j).T.astype(BF16)
    project_and_pass(1)
    project_and_pass(2)
    ring_end(0, 0)
    ring_end(0, 1)
    project_and_pass(3)
    rows_across(qplane, Q0)
    project(4, lambda i: (0, i))
    rows_y(woplane, O0)
    ended(lists, L0 + 6)

    ring_pass(2, 0)
    ended(qplane, Q0 + 9)
    for j in (0, 1):
        wt[2 * WIDE:2 * WIDE + 256, 384 * j:384 * (j + 1)] = in_order([qplane.at[0], qplane.at[1]], j).T.astype(BF16)

    def one_query(i, carried):
        query = lax.dot_general(
            wt[2 * WIDE:3 * WIDE, :], img[z * RING + i], NT, preferred_element_type=F32
        ).astype(BF16)
        both[i] = jnp.zeros((128, 2 * SEQ), BF16)
        for h in (0, 1):
            both[i, 64 * h:64 * (h + 1), SEQ * h:SEQ * (h + 1)] = query[64 * h:64 * (h + 1), :]
        third[i] = query[128:192, :]
        return carried

    lax.fori_loop(0, RING, one_query, 0)
    take(1)
    ring_pass(2, 1)
    project(2, lambda i: (1 + 2 * i, 2))
    take(2)
    tables = [jnp.sum(lists[c], axis=0) for c in (0, 1)]
    attended = lax.broadcasted_iota(I32, (32, 128), 0)

    def weight_column(querying):
        taken = jnp.zeros((32, 128), I32)
        for table in tables:
            for here, there in ((0, 1), (1, 0)):
                given = jnp.where(table[here:here + 1, :] == querying, table[2 + here:3 + here, :], 0)
                taken = taken + jnp.where(table[there:there + 1, :] == attended, given, 0)
        return jnp.sum(taken, axis=1, keepdims=True)

    column = lax.broadcasted_iota(I32, (32, 128), 1)
    by_query = [weight_column((z * RING + i) * 2 + core) for i in range(RING)]
    used = jnp.zeros((32, 128), F32)
    for i in range(RING):
        used = jnp.where((column == i) & (by_query[i] > 0), 1.0, used)
    above = jnp.where(square[1] < square[0], 1.0, 0.0)
    before = jnp.dot(above.astype(BF16), used.astype(BF16), preferred_element_type=F32)
    in_column = jnp.sum(used, axis=0, keepdims=True)
    first = jnp.zeros((1, 1), F32)
    numbers, amounts = jnp.zeros((32, 128), I32), jnp.zeros((32, 128), I32)
    for i in range(RING):
        rank = (before[:, i:i + 1] + first).astype(I32)
        here = jnp.where(by_query[i] > 0, rank, -1) == column
        numbers = numbers + jnp.where(here, attended * RING + i, 0)
        amounts = amounts + jnp.where(here, by_query[i], 0)
        first = first + in_column[:, i:i + 1]
    directions[0:1, :] = jnp.sum(numbers, axis=0, keepdims=True)
    directions[1:2, :] = jnp.sum(amounts, axis=0, keepdims=True)
    directions[2:3, :] = jnp.broadcast_to(first.astype(I32), (1, 128))
    directions[3:8, :] = jnp.zeros((5, 128), I32)
    own = jnp.sum(weight_column(chip * 2 + core).astype(F32), axis=0, keepdims=True)
    total[...] = jnp.broadcast_to(1.0 + own, (8, 128))

    ring_end(2, 0)
    ring_end(2, 1)
    project(1, lambda i: (i + 2, i + 2))
    take(3)

    for offset in (1, 2, 3):
        arrived(woplane.at[core, turn(y, 4 - offset)], O0 + 5 + offset)
    for one in started:
        one.wait_send()
    rows_x_sent(wplane, W0)
    rows_x_sent(qplane, Q0)
    rows_x_sent(woplane, O0)

    def drain(where, carried):
        pair_copy(where, where * 2 + core).wait_send()
        pair_copy(where, where * 2 + 1 - core).wait_recv()
        return carried

    lax.fori_loop(0, PLANE, drain, 0)


WINDOWS = ((0, 256, 0), (128, 384, 64), (0, 192, 0))
TOGETHER = 6


def attend_kernel(directions, kv, both, third, out, acc):
    acc[...] = jnp.zeros_like(acc)
    count = directions[2, 0]
    factor = math.log2(math.e) / 8.0

    def attention(scores):
        top = jnp.max(scores, axis=0, keepdims=True)
        expo = jnp.exp2((scores - top) * factor)
        return expo.astype(BF16), 1.0 / jnp.sum(expo, axis=0, keepdims=True)

    def several(step, carried):
        entries = [TOGETHER * step + part for part in range(TOGETHER)]
        places = [(directions[0, entry] // RING, directions[0, entry] % RING) for entry in entries]
        given = [directions[1, entry].astype(F32) for entry in entries]
        scores = [
            (
                jnp.dot(kv[t, 0:WIDE, 0:128], both[i], preferred_element_type=F32),
                jnp.dot(kv[t, 0:WIDE, 128:192], third[i], preferred_element_type=F32),
            )
            for t, i in places
        ]
        shares = [[attention(part) for part in one] for one in scores]
        found = []
        for (t, _), share, weight in zip(places, shares, given):
            for h, (low, high, _) in enumerate(WINDOWS):
                expo, scale = share[h // 2]
                one = jnp.dot(
                    kv[t, WIDE + 64 * h:WIDE + 64 * (h + 1), :], expo[:, low:high],
                    preferred_element_type=F32,
                )
                found.append((one * scale[:, low:high]).astype(BF16).astype(F32) * weight)
        for n, (_, i) in enumerate(places):
            for h in range(3):
                one = found[3 * n + h]
                acc[i, h, :, 0:one.shape[1]] += one
        return carried

    lax.fori_loop(0, (count + TOGETHER - 1) // TOGETHER, several, 0)
    for i in range(RING):
        heads = [acc[i, h][:, low:low + SEQ] for h, (_, _, low) in enumerate(WINDOWS)]
        summed = jnp.concatenate(heads, axis=0).astype(BF16)
        out[i, 0:WIDE, :] = summed[:, 0:128]
        out[i, WIDE:WIDE + 96, :] = jnp.concatenate([summed[0:96, 128:192], summed[96:192, 128:192]], axis=1)


def output_kernel(attended, woplane, total, out, wo_all, wo_both, held, send, recv):
    x, z, core = place()
    sibling = device(x, z, 1 - core)
    barrier = pltpu.get_barrier_semaphore()
    for offset in (1, 2, 3):
        pl.semaphore_signal(
            barrier, 1, device_id=device(lax.rem(x + offset, RING), z, core), device_id_type=MESH
        )
    pl.semaphore_signal(barrier, 1, device_id=sibling, device_id_type=MESH)
    pl.semaphore_wait(barrier, 4)
    copies = []
    for offset in (1, 2, 3):
        peer = lax.rem(x + offset, RING)
        one = pltpu.make_async_remote_copy(
            src_ref=attended.at[peer], dst_ref=held.at[x], send_sem=send.at[offset - 1],
            recv_sem=recv.at[offset - 1], device_id=device(peer, z, core), device_id_type=MESH,
        )
        one.start()
        copies.append(one)

    across = pltpu.make_async_remote_copy(
        src_ref=woplane.at[core], dst_ref=wo_both.at[core], send_sem=send.at[3], recv_sem=recv.at[3],
        device_id=sibling, device_id_type=MESH,
    )
    across.start()
    copies.append(across)
    wo_both[core] = woplane[core]
    pltpu.make_async_remote_copy(
        src_ref=woplane.at[core], dst_ref=wo_both.at[1 - core], send_sem=send.at[3], recv_sem=recv.at[3],
        device_id=sibling, device_id_type=MESH,
    ).wait_recv()
    for j in (0, 1):
        wo_all[384 * j:384 * (j + 1), :] = in_order([wo_both.at[0], wo_both.at[1]], j).astype(BF16)

    def product(peer, block):
        summed = jnp.concatenate(
            [block[0:WIDE, :], jnp.concatenate([block[WIDE:, 0:64], block[WIDE:, 64:128]], axis=0)], axis=1
        )
        rows = pl.ds(pl.multiple_of(peer * WIDE, WIDE), WIDE)
        return lax.dot_general(summed, wo_all[rows, :], TN, preferred_element_type=F32)

    numerator = product(x, attended[x])
    for offset in (1, 2, 3):
        peer = lax.rem(x + 4 - offset, RING)
        pltpu.make_async_remote_copy(
            src_ref=attended.at[peer], dst_ref=held.at[peer], send_sem=send.at[offset - 1],
            recv_sem=recv.at[offset - 1], device_id=device(peer, z, core), device_id_type=MESH,
        ).wait_recv()
        numerator += product(peer, held[peer])
    out[0] = (numerator / total[0:1, 0:1]).astype(BF16)
    for one in copies:
        one.wait_send()


VMEM = pl.BlockSpec(memory_space=pltpu.VMEM)
SMEM = pl.BlockSpec(memory_space=pltpu.SMEM)
HBM = pl.BlockSpec(memory_space=pltpu.HBM)


def shards(tokens, norm_gain, w_query, w_key, w_value, w_out, owner_map, pair_images, pair_count, confidence):
    kv, both, third, directions, total, woplane = pl.pallas_call(
        gather_kernel,
        out_shape=(
            jax.ShapeDtypeStruct((2 * PLANE, 2 * WIDE, SEQ), BF16),
            jax.ShapeDtypeStruct((RING, 128, 2 * SEQ), BF16),
            jax.ShapeDtypeStruct((RING, 64, SEQ), BF16),
            jax.ShapeDtypeStruct((8, 128), I32),
            jax.ShapeDtypeStruct((8, 128), F32),
            jax.ShapeDtypeStruct((2, RING, RING, ROWS, D), BF16),
        ),
        in_specs=[HBM] * 8 + [VMEM, HBM],
        out_specs=(VMEM,) * 6,
        scratch_shapes=[
            pltpu.VMEM((1, SEQ, D), BF16),
            pltpu.VMEM((D,), F32),
            pltpu.VMEM((ROWS, D), BF16),
            pltpu.VMEM((ROWS, D), BF16),
            pltpu.VMEM((ROWS, D), BF16),
            pltpu.VMEM((ROWS, D), BF16),
            pltpu.VMEM((1, 32), I32),
            pltpu.VMEM((2, 8), I32),
            pltpu.VMEM((2, 8), I32),
            pltpu.VMEM((PLANE, SEQ, D), BF16),
            pltpu.VMEM((3, 3 * WIDE, 128), BF16),
            pltpu.VMEM((2, 3, 3 * WIDE, 128), BF16),
            pltpu.VMEM((RING, ROWS, 2 * WIDE), BF16),
            pltpu.VMEM((RING, ROWS, 256), BF16),
            pltpu.VMEM((2, RING, RING, ROWS, 2 * WIDE), BF16),
            pltpu.VMEM((2, RING, RING, ROWS, 256), BF16),
            pltpu.VMEM((2, PLANE, 8, 128), I32),
            pltpu.VMEM((640, D), BF16),
            pltpu.SemaphoreType.DMA((9,)),
            pltpu.SemaphoreType.DMA((67,)),
            pltpu.SemaphoreType.DMA((67,)),
            pltpu.SemaphoreType.DMA((PLANE,)),
            pltpu.SemaphoreType.DMA((PLANE,)),
        ],
        compiler_params=pltpu.CompilerParams(
            collective_id=0, has_side_effects=True, vmem_limit_bytes=32 * 1024 * 1024
        ),
        name="gather_project",
    )(
        *[
            pltpu.with_memory_space_constraint(one, pltpu.HBM)
            for one in (tokens, norm_gain, w_query, w_key, w_value, w_out, owner_map, pair_images.T)
        ],
        pair_count.reshape(1, 1), pltpu.with_memory_space_constraint(confidence.T, pltpu.HBM),
    )
    attended = pl.pallas_call(
        attend_kernel,
        out_shape=jax.ShapeDtypeStruct((RING, WIDE + 96, 128), BF16),
        in_specs=[SMEM, VMEM, VMEM, VMEM],
        out_specs=VMEM,
        scratch_shapes=[
            pltpu.VMEM((RING, 3, 64, 256), F32),
        ],
        compiler_params=pltpu.CompilerParams(vmem_limit_bytes=32 * 1024 * 1024),
        name="attend",
    )(directions, kv, both, third)
    return pl.pallas_call(
        output_kernel,
        out_shape=jax.ShapeDtypeStruct((1, SEQ, D), BF16),
        in_specs=[VMEM] * 3,
        out_specs=VMEM,
        scratch_shapes=[
            pltpu.VMEM((D, D), BF16),
            pltpu.VMEM((2, RING, RING, ROWS, D), BF16),
            pltpu.VMEM((RING, WIDE + 96, 128), BF16),
            pltpu.SemaphoreType.DMA((4,)),
            pltpu.SemaphoreType.DMA((4,)),
        ],
        compiler_params=pltpu.CompilerParams(
            collective_id=1, has_side_effects=True, vmem_limit_bytes=32 * 1024 * 1024
        ),
        name="exchange_output",
    )(attended, woplane, total)


def solution(mesh):
    both = P(("group", "shard"))
    in_specs = (
        P(("group", "shard"), None, None),
        P(),
        P("shard", None),
        P("shard", None),
        P("shard", None),
        P("shard", None),
        P("group", None),
        P(("group", "shard"), None),
        both,
        P(("group", "shard"), None),
    )
    out_specs = P(("group", "shard"), None, None)
    return jax.shard_map(shards, mesh=mesh, in_specs=in_specs, out_specs=out_specs, check_vma=False)
```

```python
import math

import jax
import jax.numpy as jnp
from jax import lax
from jax.experimental import pallas as pl
from jax.experimental.pallas import tpu as pltpu
from jax.sharding import PartitionSpec as P

MESH = pl.DeviceIdType.MESH
F32, BF16, I32 = jnp.float32, jnp.bfloat16, jnp.int32
SEQ, D, RING, PLANE = 192, 768, 4, 16
WIDE = 192
ROWS = 24
NT = (((1,), (1,)), ((), ()))
TN = (((0,), (0,)), ((), ()))
FIRST = (0, 3, 1, 2)


def place():
    shard = lax.axis_index("shard")
    core = lax.rem(shard, 2)
    chip = lax.div(shard, 2)
    return lax.rem(chip, RING), lax.div(chip, RING), core


def device(x, z, core):
    return {"shard": (z * RING + x) * 2 + core}


def in_order(planes, j, turned=False):
    blocks = [
        (planes[c][one // RING, one % RING] if turned else planes[c][one % RING, one // RING]).astype(F32)
        for one in range(8 * j, 8 * j + 8) for c in (0, 1)
    ]
    return jnp.concatenate(blocks, axis=0)


def gather_kernel(
    tok_h, gain_h, wq_h, wk_h, wv_h, wo_h, omap_h, pimg_h, pcnt, conf_h,
    kv, both, third, directions, total, woplane,
    tok, gain, wq, wk, wv, wo, omap, pimg, conf,
    img, passed, taken, staged, staged_query, wplane, qplane, lists, wt, load, send, recv, pair_send, pair_recv,
):
    x, z, core = place()
    y = lax.axis_index("group")
    chip = z * RING + x

    def turn(value, offset):
        return lax.rem(value + offset, RING)

    def slot(ox, oz):
        return turn(z, oz) * RING + turn(x, ox)

    sibling = device(x, z, 1 - core)
    loads = [
        pltpu.make_async_copy(source, target, load.at[n])
        for n, (source, target) in enumerate((
            (tok_h, tok), (gain_h, gain), (wq_h, wq), (wk_h, wk), (wv_h, wv), (wo_h, wo),
            (omap_h, omap), (pimg_h, pimg), (conf_h, conf),
        ))
    ]
    for one in loads:
        one.start()
    barrier = pltpu.get_barrier_semaphore()
    for offset in (1, 2, 3):
        for peer in (device(turn(x, offset), z, core), device(x, turn(z, offset), core), {"group": turn(y, offset)}):
            pl.semaphore_signal(barrier, 1, device_id=peer, device_id_type=MESH)
    pl.semaphore_signal(barrier, 1, device_id=sibling, device_id_type=MESH)

    for one in loads:
        one.wait()
    values = tok[0].astype(F32)
    centred = values - jnp.mean(values, axis=-1, keepdims=True)
    variance = jnp.mean(centred * centred, axis=-1, keepdims=True)
    img[chip] = (centred * lax.rsqrt(variance + 1e-05) * gain[...].reshape(1, D)).astype(BF16)

    square = (lax.broadcasted_iota(I32, (32, 32), 0), lax.broadcasted_iota(I32, (32, 32), 1))
    owners = jnp.sum(jnp.where(square[0] == square[1], omap[...], 0), axis=1, keepdims=True)
    image = lax.broadcasted_iota(I32, (32, 8), 0)
    stored = [
        jnp.sum(jnp.where(pimg[r:r + 1, :] == image, owners, 0), axis=0, keepdims=True) for r in (0, 1)
    ]
    listed = lax.broadcasted_iota(I32, (2, 8), 1) < pcnt[...]
    entries = jnp.concatenate(stored + [jnp.where(listed, conf[...], 0), jnp.zeros((4, 8), I32)], axis=0)
    entries = jnp.concatenate([entries, jnp.zeros((8, 120), I32)], axis=1)
    lists[core, chip] = pltpu.roll(entries, 8 * chip, 1)

    @pl.when(x == y)
    def _():
        keys, values, queries = [w[...].astype(F32) for w in (wk, wv, wq)]
        for g in range(RING):
            low, high = g * WIDE, (g + 1) * WIDE
            staged[g] = jnp.concatenate([keys[:, low:high], values[:, low:high]], axis=1).astype(BF16)
            staged_query[g] = jnp.concatenate(
                [queries[:, low:high], jnp.zeros((ROWS, 64), F32)], axis=1
            ).astype(BF16)
        wplane[core, y, z] = staged[x]
        qplane[core, y, z] = staged_query[x]

    @pl.when(z == y)
    def _():
        woplane[core, y, x] = wo[...]

    pl.semaphore_wait(barrier, 10)

    started = []

    def copy(source, target, number, where):
        return pltpu.make_async_remote_copy(
            src_ref=source, dst_ref=target, send_sem=send.at[number], recv_sem=recv.at[number],
            device_id=where, device_id_type=MESH,
        )

    def start(source, target, number, where):
        one = copy(source, target, number, where)
        one.start()
        started.append(one)

    def arrived(target, number):
        copy(target, target, number, sibling).wait_recv()

    def lists_x(base):
        for offset in (1, 2, 3):
            block = lists.at[core, chip]
            start(block, block, base + offset - 1, device(turn(x, offset), z, core))

    def lists_z(base):
        for offset in (1, 2, 3):
            arrived(lists.at[core, z * RING + turn(x, 4 - offset)], base + offset - 1)
        row = lists.at[core, pl.ds(z * RING, RING)]
        for offset in (1, 2, 3):
            start(row, row, base + 2 + offset, device(x, turn(z, offset), core))

    def lists_across(base):
        for offset in (1, 2, 3):
            arrived(lists.at[core, pl.ds(turn(z, 4 - offset) * RING, RING)], base + 2 + offset)
        start(lists.at[core], lists.at[core], base + 6, sibling)

    def along(axis, offset):
        return device(turn(x, offset), z, core) if axis == 0 else device(x, turn(z, offset), core)

    def rows_first(buffer, base, outgoing, axis):
        here, there = (x, z) if axis == 0 else (z, x)
        block = buffer.at[core, y, there]

        @pl.when(here == y)
        def _():
            for offset in (1, 2, 3):
                source = block if outgoing is None else outgoing.at[turn(here, offset)]
                copy(source, block, base + offset - 1, along(axis, offset)).start()

    def rows_first_sent(buffer, base, axis):
        here, there = (x, z) if axis == 0 else (z, x)

        @pl.when(here == y)
        def _():
            for offset in (1, 2, 3):
                copy(buffer.at[core, y, there], buffer.at[core, y, there], base + offset - 1, sibling).wait_send()

    def rows_second(buffer, base, axis):
        here, there = (x, z) if axis == 0 else (z, x)
        block = buffer.at[core, y, there]

        @pl.when(here != y)
        def _():
            arrived(block, base + turn(here, 4 - y) - 1)

        for offset in (1, 2, 3):
            start(block, block, base + 2 + offset, along(1 - axis, offset))

    def rows_y(buffer, base, axis):
        there = z if axis == 0 else x
        for offset in (1, 2, 3):
            arrived(buffer.at[core, y, turn(there, 4 - offset)], base + 2 + offset)
        for offset in (1, 2, 3):
            block = buffer.at[core, y]
            start(block, block, base + 5 + offset, {"group": turn(y, offset)})

    def rows_across(buffer, base):
        for offset in (1, 2, 3):
            arrived(buffer.at[core, turn(y, 4 - offset)], base + 5 + offset)
        start(buffer.at[core], buffer.at[core], base + 9, sibling)

    def ended(buffer, number):
        arrived(buffer.at[1 - core], number)

    def piece(ring, offset, half, part=None):
        low, count = (96 * half, 96) if part is None else (96 * half + 48 * part, 48)
        where = (slot(offset, 0), slot(0, offset), slot(offset, 2))[ring]
        return img.at[where, pl.ds(low, count)]

    def ring_send(ring, offset, half, part, direction, number):
        step = (1, 3)[direction]
        peer = device(x, turn(z, step), core) if ring == 1 else device(turn(x, step), z, core)
        block = piece(ring, offset, half, part)
        start(block, block, 8 * ring + 4 * half + number + direction, peer)

    def ring_start(ring, half):
        for direction in (0, 1):
            ring_send(ring, 0, half, None, direction, 0)

    def ring_pass(ring, half):
        for direction in (0, 1):
            arrived(piece(ring, (3, 1)[direction], half), 8 * ring + 4 * half + direction)
            ring_send(ring, (3, 1)[direction], half, direction, direction, 2)

    def ring_end(ring, half):
        for direction in (0, 1):
            arrived(piece(ring, 2, half, direction), 8 * ring + 4 * half + 2 + direction)

    def pair_copy(where, row):
        return pltpu.make_async_remote_copy(
            src_ref=kv.at[row], dst_ref=kv.at[row], send_sem=pair_send.at[where],
            recv_sem=pair_recv.at[where], device_id=sibling, device_id_type=MESH,
        )

    def projected(where):
        normed = img[where]
        keys = lax.dot_general(normed, wt[0:WIDE, :], NT, preferred_element_type=F32)
        values = lax.dot_general(wt[WIDE:2 * WIDE, :], normed, NT, preferred_element_type=F32)
        kv[where * 2 + core, 0:WIDE, :] = keys.astype(BF16)
        kv[where * 2 + core, WIDE:2 * WIDE, :] = values.astype(BF16)
        pair_copy(where, where * 2 + core).start()
        return keys, values

    def project(count, offsets):
        def one(i, carried):
            projected(slot(*offsets(i)))
            return carried

        lax.fori_loop(0, count, one, 0)

    def project_and_pass(k):
        keys, values = projected(slot(FIRST[k], 0))
        passed[k - 2, 0:WIDE, :] = keys[:, 0:128].astype(BF16)
        passed[k - 2, WIDE:2 * WIDE, :] = values[:, 0:128].astype(BF16)
        passed[k - 2, 2 * WIDE:3 * WIDE, :] = jnp.concatenate(
            [keys[:, 128:WIDE], values[:, 128:WIDE]], axis=1
        ).astype(BF16)
        for direction in (0, 1):
            start(
                passed.at[k - 2], taken.at[direction, k - 2], 22 + 2 * k + direction,
                device(x, turn(z, (1, 3)[direction]), core),
            )

    def tokens_pass(k):
        block = img.at[slot(FIRST[k], 0)]
        for direction in (0, 1):
            start(block, block, 22 + 2 * k + direction, device(x, turn(z, (1, 3)[direction]), core))

    def tokens_end(k):
        for direction in (0, 1):
            arrived(img.at[slot(FIRST[k], (3, 1)[direction])], 22 + 2 * k + direction)

    def take(k):
        for direction in (0, 1):
            block = taken.at[direction, k - 2]
            arrived(block, 22 + 2 * k + direction)
            where = slot(FIRST[k], (3, 1)[direction])
            row = where * 2 + core
            kv[row, :, 0:128] = block[0:2 * WIDE, :]
            rest = block[2 * WIDE:3 * WIDE, :].astype(F32)
            kv[row, 0:WIDE, 128:WIDE] = rest[:, 0:64].astype(BF16)
            kv[row, WIDE:2 * WIDE, 128:WIDE] = rest[:, 64:128].astype(BF16)
            pair_copy(where, row).start()

    W0, L0, O0, Q0 = 30, 40, 47, 57
    rows_first(wplane, W0, staged, 0)
    rows_first(qplane, Q0, staged_query, 0)
    lists_x(L0)
    ring_start(0, 0)
    ring_start(1, 0)
    ring_start(0, 1)
    rows_first(woplane, O0, None, 1)
    rows_second(wplane, W0, 0)
    rows_second(qplane, Q0, 0)
    ring_start(1, 1)
    lists_z(L0)
    ring_pass(0, 0)
    ring_pass(1, 0)
    rows_second(woplane, O0, 1)
    rows_y(wplane, W0, 0)
    ring_pass(1, 1)
    ring_pass(0, 1)
    tokens_pass(1)
    rows_y(qplane, Q0, 0)
    ring_end(1, 0)
    ring_start(2, 0)
    rows_across(wplane, W0)
    ring_end(1, 1)
    ring_start(2, 1)
    lists_across(L0)
    rows_y(woplane, O0, 1)
    ended(lists, L0 + 6)

    tables = [jnp.sum(lists[c], axis=0) for c in (0, 1)]
    attended = lax.broadcasted_iota(I32, (32, 128), 0)

    def weight_column(querying):
        taken = jnp.zeros((32, 128), I32)
        for table in tables:
            for here, there in ((0, 1), (1, 0)):
                given = jnp.where(table[here:here + 1, :] == querying, table[2 + here:3 + here, :], 0)
                taken = taken + jnp.where(table[there:there + 1, :] == attended, given, 0)
        return jnp.sum(taken, axis=1, keepdims=True)

    column = lax.broadcasted_iota(I32, (32, 128), 1)
    by_query = [weight_column((z * RING + i) * 2 + core) for i in range(RING)]
    used = jnp.zeros((32, 128), F32)
    for i in range(RING):
        used = jnp.where((column == i) & (by_query[i] > 0), 1.0, used)
    above = jnp.where(square[1] < square[0], 1.0, 0.0)
    before = jnp.dot(above.astype(BF16), used.astype(BF16), preferred_element_type=F32)
    in_column = jnp.sum(used, axis=0, keepdims=True)
    first = jnp.zeros((1, 1), F32)
    numbers, amounts = jnp.zeros((32, 128), I32), jnp.zeros((32, 128), I32)
    for i in range(RING):
        rank = (before[:, i:i + 1] + first).astype(I32)
        here = jnp.where(by_query[i] > 0, rank, -1) == column
        numbers = numbers + jnp.where(here, attended * RING + i, 0)
        amounts = amounts + jnp.where(here, by_query[i], 0)
        first = first + in_column[:, i:i + 1]
    directions[0:1, :] = jnp.sum(numbers, axis=0, keepdims=True)
    directions[1:2, :] = jnp.sum(amounts, axis=0, keepdims=True)
    directions[2:3, :] = jnp.broadcast_to(first.astype(I32), (1, 128))
    directions[3:8, :] = jnp.zeros((5, 128), I32)
    own = jnp.sum(weight_column(chip * 2 + core).astype(F32), axis=0, keepdims=True)
    total[...] = jnp.broadcast_to(1.0 + own, (8, 128))

    ended(wplane, W0 + 9)

    for j in (0, 1):
        wt[0:2 * WIDE, 384 * j:384 * (j + 1)] = in_order([wplane.at[0], wplane.at[1]], j).T.astype(BF16)
    project_and_pass(2)
    ring_end(0, 0)
    ring_end(0, 1)
    project_and_pass(3)
    rows_across(qplane, Q0)
    project(4, lambda i: (0, i))
    project(1, lambda i: (i + 3, i))

    ring_pass(2, 0)
    ended(qplane, Q0 + 9)
    for j in (0, 1):
        wt[2 * WIDE:2 * WIDE + 256, 384 * j:384 * (j + 1)] = in_order([qplane.at[0], qplane.at[1]], j).T.astype(BF16)

    def one_query(i, carried):
        query = lax.dot_general(
            wt[2 * WIDE:3 * WIDE, :], img[z * RING + i], NT, preferred_element_type=F32
        ).astype(BF16)
        both[i] = jnp.zeros((128, 2 * SEQ), BF16)
        for h in (0, 1):
            both[i, 64 * h:64 * (h + 1), SEQ * h:SEQ * (h + 1)] = query[64 * h:64 * (h + 1), :]
        third[i] = query[128:192, :]
        return carried

    lax.fori_loop(0, RING, one_query, 0)
    tokens_end(1)
    project(2, lambda i: (i * 0 + 3, 1 + 2 * i))
    ring_pass(2, 1)
    project(2, lambda i: (1 + 2 * i, 2))
    take(2)
    ring_end(2, 0)
    ring_end(2, 1)
    project(1, lambda i: (i + 2, i + 2))
    take(3)

    for offset in (1, 2, 3):
        arrived(woplane.at[core, turn(y, 4 - offset)], O0 + 5 + offset)
    for one in started:
        one.wait_send()
    rows_first_sent(wplane, W0, 0)
    rows_first_sent(qplane, Q0, 0)
    rows_first_sent(woplane, O0, 1)

    def drain(where, carried):
        pair_copy(where, where * 2 + core).wait_send()
        pair_copy(where, where * 2 + 1 - core).wait_recv()
        return carried

    lax.fori_loop(0, PLANE, drain, 0)


WINDOWS = ((0, 256, 0), (128, 384, 64), (0, 192, 0))
TOGETHER = 6


def attend_kernel(directions, kv, both, third, out, acc):
    acc[...] = jnp.zeros_like(acc)
    count = directions[2, 0]
    factor = math.log2(math.e) / 8.0

    def attention(scores):
        top = jnp.max(scores, axis=0, keepdims=True)
        expo = jnp.exp2((scores - top) * factor)
        return expo.astype(BF16), 1.0 / jnp.sum(expo, axis=0, keepdims=True)

    def several(step, carried):
        entries = [TOGETHER * step + part for part in range(TOGETHER)]
        places = [(directions[0, entry] // RING, directions[0, entry] % RING) for entry in entries]
        given = [directions[1, entry].astype(F32) for entry in entries]
        scores = [
            (
                jnp.dot(kv[t, 0:WIDE, 0:128], both[i], preferred_element_type=F32),
                jnp.dot(kv[t, 0:WIDE, 128:192], third[i], preferred_element_type=F32),
            )
            for t, i in places
        ]
        shares = [[attention(part) for part in one] for one in scores]
        found = []
        for (t, _), share, weight in zip(places, shares, given):
            for h, (low, high, _) in enumerate(WINDOWS):
                expo, scale = share[h // 2]
                one = jnp.dot(
                    kv[t, WIDE + 64 * h:WIDE + 64 * (h + 1), :], expo[:, low:high],
                    preferred_element_type=F32,
                )
                found.append((one * scale[:, low:high]).astype(BF16).astype(F32) * weight)
        for n, (_, i) in enumerate(places):
            for h in range(3):
                one = found[3 * n + h]
                acc[i, h, :, 0:one.shape[1]] += one
        return carried

    lax.fori_loop(0, (count + TOGETHER - 1) // TOGETHER, several, 0)
    for i in range(RING):
        heads = [acc[i, h][:, low:low + SEQ] for h, (_, _, low) in enumerate(WINDOWS)]
        summed = jnp.concatenate(heads, axis=0).astype(BF16)
        out[i, 0:WIDE, :] = summed[:, 0:128]
        out[i, WIDE:WIDE + 96, :] = jnp.concatenate([summed[0:96, 128:192], summed[96:192, 128:192]], axis=1)


def output_kernel(attended, woplane, total, out, wo_all, wo_both, held, send, recv):
    x, z, core = place()
    sibling = device(x, z, 1 - core)
    barrier = pltpu.get_barrier_semaphore()
    for offset in (1, 2, 3):
        pl.semaphore_signal(
            barrier, 1, device_id=device(lax.rem(x + offset, RING), z, core), device_id_type=MESH
        )
    pl.semaphore_signal(barrier, 1, device_id=sibling, device_id_type=MESH)
    pl.semaphore_wait(barrier, 4)
    copies = []
    for offset in (2, 1, 3):
        peer = lax.rem(x + offset, RING)
        one = pltpu.make_async_remote_copy(
            src_ref=attended.at[peer], dst_ref=held.at[x], send_sem=send.at[offset - 1],
            recv_sem=recv.at[offset - 1], device_id=device(peer, z, core), device_id_type=MESH,
        )
        one.start()
        copies.append(one)

    across = pltpu.make_async_remote_copy(
        src_ref=woplane.at[core], dst_ref=wo_both.at[core], send_sem=send.at[3], recv_sem=recv.at[3],
        device_id=sibling, device_id_type=MESH,
    )
    across.start()
    copies.append(across)
    wo_both[core] = woplane[core]
    pltpu.make_async_remote_copy(
        src_ref=woplane.at[core], dst_ref=wo_both.at[1 - core], send_sem=send.at[3], recv_sem=recv.at[3],
        device_id=sibling, device_id_type=MESH,
    ).wait_recv()
    for j in (0, 1):
        wo_all[384 * j:384 * (j + 1), :] = in_order([wo_both.at[0], wo_both.at[1]], j, True).astype(BF16)

    def product(peer, block):
        summed = jnp.concatenate(
            [block[0:WIDE, :], jnp.concatenate([block[WIDE:, 0:64], block[WIDE:, 64:128]], axis=0)], axis=1
        )
        rows = pl.ds(pl.multiple_of(peer * WIDE, WIDE), WIDE)
        return lax.dot_general(summed, wo_all[rows, :], TN, preferred_element_type=F32)

    numerator = product(x, attended[x])
    for offset in (1, 3, 2):
        peer = lax.rem(x + 4 - offset, RING)
        pltpu.make_async_remote_copy(
            src_ref=attended.at[peer], dst_ref=held.at[peer], send_sem=send.at[offset - 1],
            recv_sem=recv.at[offset - 1], device_id=device(peer, z, core), device_id_type=MESH,
        ).wait_recv()
        numerator += product(peer, held[peer])
    out[0] = (numerator * (1.0 / total[0:1, 0:1])).astype(BF16)
    for one in copies:
        one.wait_send()


VMEM = pl.BlockSpec(memory_space=pltpu.VMEM)
SMEM = pl.BlockSpec(memory_space=pltpu.SMEM)
HBM = pl.BlockSpec(memory_space=pltpu.HBM)


def shards(tokens, norm_gain, w_query, w_key, w_value, w_out, owner_map, pair_images, pair_count, confidence):
    kv, both, third, directions, total, woplane = pl.pallas_call(
        gather_kernel,
        out_shape=(
            jax.ShapeDtypeStruct((2 * PLANE, 2 * WIDE, SEQ), BF16),
            jax.ShapeDtypeStruct((RING, 128, 2 * SEQ), BF16),
            jax.ShapeDtypeStruct((RING, 64, SEQ), BF16),
            jax.ShapeDtypeStruct((8, 128), I32),
            jax.ShapeDtypeStruct((8, 128), F32),
            jax.ShapeDtypeStruct((2, RING, RING, ROWS, D), BF16),
        ),
        in_specs=[HBM] * 8 + [VMEM, HBM],
        out_specs=(VMEM,) * 6,
        scratch_shapes=[
            pltpu.VMEM((1, SEQ, D), BF16),
            pltpu.VMEM((D,), F32),
            pltpu.VMEM((ROWS, D), BF16),
            pltpu.VMEM((ROWS, D), BF16),
            pltpu.VMEM((ROWS, D), BF16),
            pltpu.VMEM((ROWS, D), BF16),
            pltpu.VMEM((1, 32), I32),
            pltpu.VMEM((2, 8), I32),
            pltpu.VMEM((2, 8), I32),
            pltpu.VMEM((PLANE, SEQ, D), BF16),
            pltpu.VMEM((2, 3 * WIDE, 128), BF16),
            pltpu.VMEM((2, 2, 3 * WIDE, 128), BF16),
            pltpu.VMEM((RING, ROWS, 2 * WIDE), BF16),
            pltpu.VMEM((RING, ROWS, 256), BF16),
            pltpu.VMEM((2, RING, RING, ROWS, 2 * WIDE), BF16),
            pltpu.VMEM((2, RING, RING, ROWS, 256), BF16),
            pltpu.VMEM((2, PLANE, 8, 128), I32),
            pltpu.VMEM((640, D), BF16),
            pltpu.SemaphoreType.DMA((9,)),
            pltpu.SemaphoreType.DMA((67,)),
            pltpu.SemaphoreType.DMA((67,)),
            pltpu.SemaphoreType.DMA((PLANE,)),
            pltpu.SemaphoreType.DMA((PLANE,)),
        ],
        compiler_params=pltpu.CompilerParams(
            collective_id=0, has_side_effects=True, vmem_limit_bytes=32 * 1024 * 1024
        ),
        name="gather_project",
    )(
        *[
            pltpu.with_memory_space_constraint(one, pltpu.HBM)
            for one in (tokens, norm_gain, w_query, w_key, w_value, w_out, owner_map, pair_images.T)
        ],
        pair_count.reshape(1, 1), pltpu.with_memory_space_constraint(confidence.T, pltpu.HBM),
    )
    attended = pl.pallas_call(
        attend_kernel,
        out_shape=jax.ShapeDtypeStruct((RING, WIDE + 96, 128), BF16),
        in_specs=[SMEM, VMEM, VMEM, VMEM],
        out_specs=VMEM,
        scratch_shapes=[
            pltpu.VMEM((RING, 3, 64, 256), F32),
        ],
        compiler_params=pltpu.CompilerParams(vmem_limit_bytes=32 * 1024 * 1024),
        name="attend",
    )(directions, kv, both, third)
    return pl.pallas_call(
        output_kernel,
        out_shape=jax.ShapeDtypeStruct((1, SEQ, D), BF16),
        in_specs=[VMEM] * 3,
        out_specs=VMEM,
        scratch_shapes=[
            pltpu.VMEM((D, D), BF16),
            pltpu.VMEM((2, RING, RING, ROWS, D), BF16),
            pltpu.VMEM((RING, WIDE + 96, 128), BF16),
            pltpu.SemaphoreType.DMA((4,)),
            pltpu.SemaphoreType.DMA((4,)),
        ],
        compiler_params=pltpu.CompilerParams(
            collective_id=1, has_side_effects=True, vmem_limit_bytes=32 * 1024 * 1024
        ),
        name="exchange_output",
    )(attended, woplane, total)


def solution(mesh):
    both = P(("group", "shard"))
    in_specs = (
        P(("group", "shard"), None, None),
        P(),
        P("shard", None),
        P("shard", None),
        P("shard", None),
        P("shard", None),
        P("group", None),
        P(("group", "shard"), None),
        both,
        P(("group", "shard"), None),
    )
    out_specs = P(("group", "shard"), None, None)
    return jax.shard_map(shards, mesh=mesh, in_specs=in_specs, out_specs=out_specs, check_vma=False)
```

```python
import math

import jax
import jax.numpy as jnp
from jax import lax
from jax.experimental import pallas as pl
from jax.experimental.pallas import tpu as pltpu
from jax.sharding import PartitionSpec as P

MESH = pl.DeviceIdType.MESH
F32, BF16, I32 = jnp.float32, jnp.bfloat16, jnp.int32
SEQ, D, RING, PLANE = 192, 768, 4, 16
WIDE = 192
ROWS = 24
NT = (((1,), (1,)), ((), ()))
TN = (((0,), (0,)), ((), ()))
FIRST = (0, 3, 1, 2)


def place():
    shard = lax.axis_index("shard")
    core = lax.rem(shard, 2)
    chip = lax.div(shard, 2)
    return lax.rem(chip, RING), lax.div(chip, RING), core


def device(x, z, core):
    return {"shard": (z * RING + x) * 2 + core}


def in_order(planes, j, turned=False):
    blocks = [
        (planes[c][one // RING, one % RING] if turned else planes[c][one % RING, one // RING]).astype(F32)
        for one in range(8 * j, 8 * j + 8) for c in (0, 1)
    ]
    return jnp.concatenate(blocks, axis=0)


def gather_kernel(
    tok_h, gain_h, wq_h, wk_h, wv_h, wo_h, omap_h, pimg_h, pcnt, conf_h,
    kv, both, third, directions, total, woplane,
    tok, gain, wq, wk, wv, wo, omap, pimg, conf,
    img, passed, taken, staged, staged_query, wplane, qplane, lists, wt, load, send, recv, pair_send, pair_recv,
):
    x, z, core = place()
    y = lax.axis_index("group")
    chip = z * RING + x

    def turn(value, offset):
        return lax.rem(value + offset, RING)

    def slot(ox, oz):
        return turn(z, oz) * RING + turn(x, ox)

    sibling = device(x, z, 1 - core)
    loads = [
        pltpu.make_async_copy(source, target, load.at[n])
        for n, (source, target) in enumerate((
            (tok_h, tok), (gain_h, gain), (wq_h, wq), (wk_h, wk), (wv_h, wv), (wo_h, wo),
            (omap_h, omap), (pimg_h, pimg), (conf_h, conf),
        ))
    ]
    for one in loads:
        one.start()
    barrier = pltpu.get_barrier_semaphore()
    for offset in (1, 2, 3):
        for peer in (device(turn(x, offset), z, core), device(x, turn(z, offset), core), {"group": turn(y, offset)}):
            pl.semaphore_signal(barrier, 1, device_id=peer, device_id_type=MESH)
    pl.semaphore_signal(barrier, 1, device_id=sibling, device_id_type=MESH)

    for one in loads:
        one.wait()
    values = tok[0].astype(F32)
    centred = values - jnp.mean(values, axis=-1, keepdims=True)
    variance = jnp.mean(centred * centred, axis=-1, keepdims=True)
    img[chip] = (centred * lax.rsqrt(variance + 1e-05) * gain[...].reshape(1, D)).astype(BF16)

    square = (lax.broadcasted_iota(I32, (32, 32), 0), lax.broadcasted_iota(I32, (32, 32), 1))
    owners = jnp.sum(jnp.where(square[0] == square[1], omap[...], 0), axis=1, keepdims=True)
    image = lax.broadcasted_iota(I32, (32, 8), 0)
    stored = [
        jnp.sum(jnp.where(pimg[r:r + 1, :] == image, owners, 0), axis=0, keepdims=True) for r in (0, 1)
    ]
    listed = lax.broadcasted_iota(I32, (2, 8), 1) < pcnt[...]
    entries = jnp.concatenate(stored + [jnp.where(listed, conf[...], 0), jnp.zeros((4, 8), I32)], axis=0)
    entries = jnp.concatenate([entries, jnp.zeros((8, 120), I32)], axis=1)
    lists[core, chip] = pltpu.roll(entries, 8 * chip, 1)

    @pl.when(x == y)
    def _():
        keys, values, queries = [w[...].astype(F32) for w in (wk, wv, wq)]
        for g in range(RING):
            low, high = g * WIDE, (g + 1) * WIDE
            staged[g] = jnp.concatenate([keys[:, low:high], values[:, low:high]], axis=1).astype(BF16)
            staged_query[g] = jnp.concatenate(
                [queries[:, low:high], jnp.zeros((ROWS, 64), F32)], axis=1
            ).astype(BF16)
        wplane[core, y, z] = staged[x]
        qplane[core, y, z] = staged_query[x]

    @pl.when(z == y)
    def _():
        woplane[core, y, x] = wo[...]

    pl.semaphore_wait(barrier, 10)

    started = []

    def copy(source, target, number, where):
        return pltpu.make_async_remote_copy(
            src_ref=source, dst_ref=target, send_sem=send.at[number], recv_sem=recv.at[number],
            device_id=where, device_id_type=MESH,
        )

    def start(source, target, number, where):
        one = copy(source, target, number, where)
        one.start()
        started.append(one)

    def arrived(target, number):
        copy(target, target, number, sibling).wait_recv()

    def lists_x(base):
        for offset in (1, 2, 3):
            block = lists.at[core, chip]
            start(block, block, base + offset - 1, device(turn(x, offset), z, core))

    def lists_z(base):
        for offset in (1, 2, 3):
            arrived(lists.at[core, z * RING + turn(x, 4 - offset)], base + offset - 1)
        row = lists.at[core, pl.ds(z * RING, RING)]
        for offset in (1, 2, 3):
            start(row, row, base + 2 + offset, device(x, turn(z, offset), core))

    def lists_across(base):
        for offset in (1, 2, 3):
            arrived(lists.at[core, pl.ds(turn(z, 4 - offset) * RING, RING)], base + 2 + offset)
        start(lists.at[core], lists.at[core], base + 6, sibling)

    def along(axis, offset):
        return device(turn(x, offset), z, core) if axis == 0 else device(x, turn(z, offset), core)

    def rows_first(buffer, base, outgoing, axis):
        here, there = (x, z) if axis == 0 else (z, x)
        block = buffer.at[core, y, there]

        @pl.when(here == y)
        def _():
            for offset in (1, 2, 3):
                source = block if outgoing is None else outgoing.at[turn(here, offset)]
                copy(source, block, base + offset - 1, along(axis, offset)).start()

    def rows_first_sent(buffer, base, axis):
        here, there = (x, z) if axis == 0 else (z, x)

        @pl.when(here == y)
        def _():
            for offset in (1, 2, 3):
                copy(buffer.at[core, y, there], buffer.at[core, y, there], base + offset - 1, sibling).wait_send()

    def rows_second(buffer, base, axis):
        here, there = (x, z) if axis == 0 else (z, x)
        block = buffer.at[core, y, there]

        @pl.when(here != y)
        def _():
            arrived(block, base + turn(here, 4 - y) - 1)

        for offset in (1, 2, 3):
            start(block, block, base + 2 + offset, along(1 - axis, offset))

    def rows_y(buffer, base, axis):
        there = z if axis == 0 else x
        for offset in (1, 2, 3):
            arrived(buffer.at[core, y, turn(there, 4 - offset)], base + 2 + offset)
        for offset in (1, 2, 3):
            block = buffer.at[core, y]
            start(block, block, base + 5 + offset, {"group": turn(y, offset)})

    def rows_across(buffer, base):
        for offset in (1, 2, 3):
            arrived(buffer.at[core, turn(y, 4 - offset)], base + 5 + offset)
        start(buffer.at[core], buffer.at[core], base + 9, sibling)

    def ended(buffer, number):
        arrived(buffer.at[1 - core], number)

    def piece(ring, offset, half, part=None):
        low, count = (96 * half, 96) if part is None else (96 * half + 48 * part, 48)
        where = (slot(offset, 0), slot(0, offset), slot(offset, 2))[ring]
        return img.at[where, pl.ds(low, count)]

    def ring_send(ring, offset, half, part, direction, number):
        step = (1, 3)[direction]
        peer = device(x, turn(z, step), core) if ring == 1 else device(turn(x, step), z, core)
        block = piece(ring, offset, half, part)
        start(block, block, 8 * ring + 4 * half + number + direction, peer)

    def ring_start(ring, half):
        for direction in (0, 1):
            ring_send(ring, 0, half, None, direction, 0)

    def ring_pass(ring, half):
        for direction in (0, 1):
            arrived(piece(ring, (3, 1)[direction], half), 8 * ring + 4 * half + direction)
            ring_send(ring, (3, 1)[direction], half, direction, direction, 2)

    def ring_end(ring, half):
        for direction in (0, 1):
            arrived(piece(ring, 2, half, direction), 8 * ring + 4 * half + 2 + direction)

    def pair_copy(where, row):
        return pltpu.make_async_remote_copy(
            src_ref=kv.at[row], dst_ref=kv.at[row], send_sem=pair_send.at[where],
            recv_sem=pair_recv.at[where], device_id=sibling, device_id_type=MESH,
        )

    def projected(where):
        normed = img[where]
        keys = lax.dot_general(normed, wt[0:WIDE, :], NT, preferred_element_type=F32)
        values = lax.dot_general(wt[WIDE:2 * WIDE, :], normed, NT, preferred_element_type=F32)
        kv[where * 2 + core, 0:WIDE, :] = keys.astype(BF16)
        kv[where * 2 + core, WIDE:2 * WIDE, :] = values.astype(BF16)
        pair_copy(where, where * 2 + core).start()
        return keys, values

    def project(count, offsets):
        def one(i, carried):
            projected(slot(*offsets(i)))
            return carried

        lax.fori_loop(0, count, one, 0)

    def project_and_pass(k):
        keys, values = projected(slot(FIRST[k], 0))
        passed[k - 2, 0:WIDE, :] = keys[:, 0:128].astype(BF16)
        passed[k - 2, WIDE:2 * WIDE, :] = values[:, 0:128].astype(BF16)
        passed[k - 2, 2 * WIDE:3 * WIDE, :] = jnp.concatenate(
            [keys[:, 128:WIDE], values[:, 128:WIDE]], axis=1
        ).astype(BF16)
        for direction in (0, 1):
            start(
                passed.at[k - 2], taken.at[direction, k - 2], 22 + 2 * k + direction,
                device(x, turn(z, (1, 3)[direction]), core),
            )

    def tokens_pass(k):
        block = img.at[slot(FIRST[k], 0)]
        for direction in (0, 1):
            start(block, block, 22 + 2 * k + direction, device(x, turn(z, (1, 3)[direction]), core))

    def tokens_end(k):
        for direction in (0, 1):
            arrived(img.at[slot(FIRST[k], (3, 1)[direction])], 22 + 2 * k + direction)

    def take(k):
        for direction in (0, 1):
            block = taken.at[direction, k - 2]
            arrived(block, 22 + 2 * k + direction)
            where = slot(FIRST[k], (3, 1)[direction])
            row = where * 2 + core
            kv[row, :, 0:128] = block[0:2 * WIDE, :]
            rest = block[2 * WIDE:3 * WIDE, :].astype(F32)
            kv[row, 0:WIDE, 128:WIDE] = rest[:, 0:64].astype(BF16)
            kv[row, WIDE:2 * WIDE, 128:WIDE] = rest[:, 64:128].astype(BF16)
            pair_copy(where, row).start()

    W0, L0, O0, Q0 = 30, 40, 47, 57
    rows_first(wplane, W0, staged, 0)
    rows_first(qplane, Q0, staged_query, 0)
    lists_x(L0)
    ring_start(0, 0)
    ring_start(1, 0)
    ring_start(0, 1)
    rows_first(woplane, O0, None, 1)
    rows_second(wplane, W0, 0)
    ring_start(1, 1)
    rows_second(qplane, Q0, 0)
    lists_z(L0)
    ring_pass(0, 0)
    ring_pass(1, 0)
    rows_second(woplane, O0, 1)
    rows_y(wplane, W0, 0)
    ring_pass(1, 1)
    ring_pass(0, 1)
    tokens_pass(1)
    rows_y(qplane, Q0, 0)
    ring_end(1, 0)
    ring_start(2, 0)
    rows_across(wplane, W0)
    ring_end(1, 1)
    ring_start(2, 1)
    lists_across(L0)
    rows_y(woplane, O0, 1)
    ended(lists, L0 + 6)

    tables = [jnp.sum(lists[c], axis=0) for c in (0, 1)]
    attended = lax.broadcasted_iota(I32, (32, 128), 0)

    def weight_column(querying):
        taken = jnp.zeros((32, 128), I32)
        for table in tables:
            for here, there in ((0, 1), (1, 0)):
                given = jnp.where(table[here:here + 1, :] == querying, table[2 + here:3 + here, :], 0)
                taken = taken + jnp.where(table[there:there + 1, :] == attended, given, 0)
        return jnp.sum(taken, axis=1, keepdims=True)

    column = lax.broadcasted_iota(I32, (32, 128), 1)
    by_query = [weight_column((z * RING + i) * 2 + core) for i in range(RING)]
    used = jnp.zeros((32, 128), F32)
    for i in range(RING):
        used = jnp.where((column == i) & (by_query[i] > 0), 1.0, used)
    above = jnp.where(square[1] < square[0], 1.0, 0.0)
    before = jnp.dot(above.astype(BF16), used.astype(BF16), preferred_element_type=F32)
    in_column = jnp.sum(used, axis=0, keepdims=True)
    first = jnp.zeros((1, 1), F32)
    numbers, amounts = jnp.zeros((32, 128), I32), jnp.zeros((32, 128), I32)
    for i in range(RING):
        rank = (before[:, i:i + 1] + first).astype(I32)
        here = jnp.where(by_query[i] > 0, rank, -1) == column
        numbers = numbers + jnp.where(here, attended * RING + i, 0)
        amounts = amounts + jnp.where(here, by_query[i], 0)
        first = first + in_column[:, i:i + 1]
    directions[0:1, :] = jnp.sum(numbers, axis=0, keepdims=True)
    directions[1:2, :] = jnp.sum(amounts, axis=0, keepdims=True)
    directions[2:3, :] = jnp.broadcast_to(first.astype(I32), (1, 128))
    directions[3:8, :] = jnp.zeros((5, 128), I32)
    own = jnp.sum(weight_column(chip * 2 + core).astype(F32), axis=0, keepdims=True)
    total[...] = jnp.broadcast_to(1.0 + own, (8, 128))

    ended(wplane, W0 + 9)

    for j in (0, 1):
        wt[0:2 * WIDE, 384 * j:384 * (j + 1)] = in_order([wplane.at[0], wplane.at[1]], j).T.astype(BF16)
    project_and_pass(2)
    ring_end(0, 0)
    ring_end(0, 1)
    project_and_pass(3)
    rows_across(qplane, Q0)
    project(4, lambda i: (0, i))
    project(1, lambda i: (i + 3, i))

    ring_pass(2, 0)
    ended(qplane, Q0 + 9)
    for j in (0, 1):
        wt[2 * WIDE:2 * WIDE + 256, 384 * j:384 * (j + 1)] = in_order([qplane.at[0], qplane.at[1]], j).T.astype(BF16)

    def one_query(i, carried):
        query = lax.dot_general(
            wt[2 * WIDE:3 * WIDE, :], img[z * RING + i], NT, preferred_element_type=F32
        ).astype(BF16)
        both[i] = jnp.zeros((128, 2 * SEQ), BF16)
        for h in (0, 1):
            both[i, 64 * h:64 * (h + 1), SEQ * h:SEQ * (h + 1)] = query[64 * h:64 * (h + 1), :]
        third[i] = query[128:192, :]
        return carried

    lax.fori_loop(0, RING, one_query, 0)
    tokens_end(1)
    project(2, lambda i: (i * 0 + 3, 1 + 2 * i))
    ring_pass(2, 1)
    project(2, lambda i: (1 + 2 * i, 2))
    take(2)
    take(3)
    ring_end(2, 0)
    ring_end(2, 1)
    project(1, lambda i: (i + 2, i + 2))

    for offset in (1, 2, 3):
        arrived(woplane.at[core, turn(y, 4 - offset)], O0 + 5 + offset)
    for one in started:
        one.wait_send()
    rows_first_sent(wplane, W0, 0)
    rows_first_sent(qplane, Q0, 0)
    rows_first_sent(woplane, O0, 1)

    def drain(where, carried):
        pair_copy(where, where * 2 + core).wait_send()
        pair_copy(where, where * 2 + 1 - core).wait_recv()
        return carried

    lax.fori_loop(0, PLANE, drain, 0)


WINDOWS = ((0, 256, 0), (128, 384, 64), (0, 192, 0))
TOGETHER = 6


def attend_kernel(directions, kv, both, third, out, acc):
    acc[...] = jnp.zeros_like(acc)
    count = directions[2, 0]
    factor = math.log2(math.e) / 8.0

    def attention(scores):
        top = jnp.max(scores, axis=0, keepdims=True)
        expo = jnp.exp2((scores - top) * factor)
        return expo.astype(BF16), 1.0 / jnp.sum(expo, axis=0, keepdims=True)

    def several(step, carried):
        entries = [TOGETHER * step + part for part in range(TOGETHER)]
        places = [(directions[0, entry] // RING, directions[0, entry] % RING) for entry in entries]
        given = [directions[1, entry].astype(F32) for entry in entries]
        scores = [
            (
                jnp.dot(kv[t, 0:WIDE, 0:128], both[i], preferred_element_type=F32),
                jnp.dot(kv[t, 0:WIDE, 128:192], third[i], preferred_element_type=F32),
            )
            for t, i in places
        ]
        shares = [[attention(part) for part in one] for one in scores]
        found = []
        for (t, _), share, weight in zip(places, shares, given):
            for h, (low, high, _) in enumerate(WINDOWS):
                expo, scale = share[h // 2]
                one = jnp.dot(
                    kv[t, WIDE + 64 * h:WIDE + 64 * (h + 1), :], expo[:, low:high],
                    preferred_element_type=F32,
                )
                found.append((one * scale[:, low:high]).astype(BF16).astype(F32) * weight)
        for n, (_, i) in enumerate(places):
            for h in range(3):
                one = found[3 * n + h]
                acc[i, h, :, 0:one.shape[1]] += one
        return carried

    lax.fori_loop(0, (count + TOGETHER - 1) // TOGETHER, several, 0)
    for i in range(RING):
        heads = [acc[i, h][:, low:low + SEQ] for h, (_, _, low) in enumerate(WINDOWS)]
        summed = jnp.concatenate(heads, axis=0).astype(BF16)
        out[i, 0:WIDE, :] = summed[:, 0:128]
        out[i, WIDE:WIDE + 96, :] = jnp.concatenate([summed[0:96, 128:192], summed[96:192, 128:192]], axis=1)


def output_kernel(attended, woplane, total, out, wo_all, wo_both, held, send, recv):
    x, z, core = place()
    sibling = device(x, z, 1 - core)
    barrier = pltpu.get_barrier_semaphore()
    for offset in (1, 2, 3):
        pl.semaphore_signal(
            barrier, 1, device_id=device(lax.rem(x + offset, RING), z, core), device_id_type=MESH
        )
    pl.semaphore_signal(barrier, 1, device_id=sibling, device_id_type=MESH)
    pl.semaphore_wait(barrier, 4)
    copies = []
    for offset in (2, 1, 3):
        peer = lax.rem(x + offset, RING)
        one = pltpu.make_async_remote_copy(
            src_ref=attended.at[peer], dst_ref=held.at[x], send_sem=send.at[offset - 1],
            recv_sem=recv.at[offset - 1], device_id=device(peer, z, core), device_id_type=MESH,
        )
        one.start()
        copies.append(one)

    across = pltpu.make_async_remote_copy(
        src_ref=woplane.at[core], dst_ref=wo_both.at[core], send_sem=send.at[3], recv_sem=recv.at[3],
        device_id=sibling, device_id_type=MESH,
    )
    across.start()
    copies.append(across)
    wo_both[core] = woplane[core]
    pltpu.make_async_remote_copy(
        src_ref=woplane.at[core], dst_ref=wo_both.at[1 - core], send_sem=send.at[3], recv_sem=recv.at[3],
        device_id=sibling, device_id_type=MESH,
    ).wait_recv()
    for j in (0, 1):
        wo_all[384 * j:384 * (j + 1), :] = in_order([wo_both.at[0], wo_both.at[1]], j, True).astype(BF16)

    def product(peer, block):
        summed = jnp.concatenate(
            [block[0:WIDE, :], jnp.concatenate([block[WIDE:, 0:64], block[WIDE:, 64:128]], axis=0)], axis=1
        )
        rows = pl.ds(pl.multiple_of(peer * WIDE, WIDE), WIDE)
        return lax.dot_general(summed, wo_all[rows, :], TN, preferred_element_type=F32)

    numerator = product(x, attended[x])
    for offset in (1, 3, 2):
        peer = lax.rem(x + 4 - offset, RING)
        pltpu.make_async_remote_copy(
            src_ref=attended.at[peer], dst_ref=held.at[peer], send_sem=send.at[offset - 1],
            recv_sem=recv.at[offset - 1], device_id=device(peer, z, core), device_id_type=MESH,
        ).wait_recv()
        numerator += product(peer, held[peer])
    out[0] = (numerator * (1.0 / total[0:1, 0:1])).astype(BF16)
    for one in copies:
        one.wait_send()


VMEM = pl.BlockSpec(memory_space=pltpu.VMEM)
SMEM = pl.BlockSpec(memory_space=pltpu.SMEM)
HBM = pl.BlockSpec(memory_space=pltpu.HBM)


def shards(tokens, norm_gain, w_query, w_key, w_value, w_out, owner_map, pair_images, pair_count, confidence):
    kv, both, third, directions, total, woplane = pl.pallas_call(
        gather_kernel,
        out_shape=(
            jax.ShapeDtypeStruct((2 * PLANE, 2 * WIDE, SEQ), BF16),
            jax.ShapeDtypeStruct((RING, 128, 2 * SEQ), BF16),
            jax.ShapeDtypeStruct((RING, 64, SEQ), BF16),
            jax.ShapeDtypeStruct((8, 128), I32),
            jax.ShapeDtypeStruct((8, 128), F32),
            jax.ShapeDtypeStruct((2, RING, RING, ROWS, D), BF16),
        ),
        in_specs=[HBM] * 8 + [VMEM, HBM],
        out_specs=(VMEM,) * 6,
        scratch_shapes=[
            pltpu.VMEM((1, SEQ, D), BF16),
            pltpu.VMEM((D,), F32),
            pltpu.VMEM((ROWS, D), BF16),
            pltpu.VMEM((ROWS, D), BF16),
            pltpu.VMEM((ROWS, D), BF16),
            pltpu.VMEM((ROWS, D), BF16),
            pltpu.VMEM((1, 32), I32),
            pltpu.VMEM((2, 8), I32),
            pltpu.VMEM((2, 8), I32),
            pltpu.VMEM((PLANE, SEQ, D), BF16),
            pltpu.VMEM((2, 3 * WIDE, 128), BF16),
            pltpu.VMEM((2, 2, 3 * WIDE, 128), BF16),
            pltpu.VMEM((RING, ROWS, 2 * WIDE), BF16),
            pltpu.VMEM((RING, ROWS, 256), BF16),
            pltpu.VMEM((2, RING, RING, ROWS, 2 * WIDE), BF16),
            pltpu.VMEM((2, RING, RING, ROWS, 256), BF16),
            pltpu.VMEM((2, PLANE, 8, 128), I32),
            pltpu.VMEM((640, D), BF16),
            pltpu.SemaphoreType.DMA((9,)),
            pltpu.SemaphoreType.DMA((67,)),
            pltpu.SemaphoreType.DMA((67,)),
            pltpu.SemaphoreType.DMA((PLANE,)),
            pltpu.SemaphoreType.DMA((PLANE,)),
        ],
        compiler_params=pltpu.CompilerParams(
            collective_id=0, has_side_effects=True, vmem_limit_bytes=32 * 1024 * 1024
        ),
        name="gather_project",
    )(
        *[
            pltpu.with_memory_space_constraint(one, pltpu.HBM)
            for one in (tokens, norm_gain, w_query, w_key, w_value, w_out, owner_map, pair_images.T)
        ],
        pair_count.reshape(1, 1), pltpu.with_memory_space_constraint(confidence.T, pltpu.HBM),
    )
    attended = pl.pallas_call(
        attend_kernel,
        out_shape=jax.ShapeDtypeStruct((RING, WIDE + 96, 128), BF16),
        in_specs=[SMEM, VMEM, VMEM, VMEM],
        out_specs=VMEM,
        scratch_shapes=[
            pltpu.VMEM((RING, 3, 64, 256), F32),
        ],
        compiler_params=pltpu.CompilerParams(vmem_limit_bytes=32 * 1024 * 1024),
        name="attend",
    )(directions, kv, both, third)
    return pl.pallas_call(
        output_kernel,
        out_shape=jax.ShapeDtypeStruct((1, SEQ, D), BF16),
        in_specs=[VMEM] * 3,
        out_specs=VMEM,
        scratch_shapes=[
            pltpu.VMEM((D, D), BF16),
            pltpu.VMEM((2, RING, RING, ROWS, D), BF16),
            pltpu.VMEM((RING, WIDE + 96, 128), BF16),
            pltpu.SemaphoreType.DMA((4,)),
            pltpu.SemaphoreType.DMA((4,)),
        ],
        compiler_params=pltpu.CompilerParams(
            collective_id=1, has_side_effects=True, vmem_limit_bytes=32 * 1024 * 1024
        ),
        name="exchange_output",
    )(attended, woplane, total)


def solution(mesh):
    both = P(("group", "shard"))
    in_specs = (
        P(("group", "shard"), None, None),
        P(),
        P("shard", None),
        P("shard", None),
        P("shard", None),
        P("shard", None),
        P("group", None),
        P(("group", "shard"), None),
        both,
        P(("group", "shard"), None),
    )
    out_specs = P(("group", "shard"), None, None)
    return jax.shard_map(shards, mesh=mesh, in_specs=in_specs, out_specs=out_specs, check_vma=False)
```

```python
import math

import jax
import jax.numpy as jnp
from jax import lax
from jax.experimental import pallas as pl
from jax.experimental.pallas import tpu as pltpu
from jax.sharding import PartitionSpec as P

MESH = pl.DeviceIdType.MESH
F32, BF16, I32 = jnp.float32, jnp.bfloat16, jnp.int32
SEQ, D, RING, PLANE = 192, 768, 4, 16
WIDE = 192
ROWS = 24
NT = (((1,), (1,)), ((), ()))
TN = (((0,), (0,)), ((), ()))
FIRST = (0, 3, 1, 2)


def place():
    shard = lax.axis_index("shard")
    core = lax.rem(shard, 2)
    chip = lax.div(shard, 2)
    return lax.rem(chip, RING), lax.div(chip, RING), core


def device(x, z, core):
    return {"shard": (z * RING + x) * 2 + core}


def in_order(planes, j, turned=False):
    blocks = [
        (planes[c][one // RING, one % RING] if turned else planes[c][one % RING, one // RING]).astype(F32)
        for one in range(8 * j, 8 * j + 8) for c in (0, 1)
    ]
    return jnp.concatenate(blocks, axis=0)


def gather_kernel(
    tok_h, gain_h, wq_h, wk_h, wv_h, wo_h, omap_h, pimg_h, pcnt, conf_h,
    kv, both, third, directions, total, woplane,
    tok, gain, wq, wk, wv, wo, omap, pimg, conf,
    img, passed, taken, staged, staged_query, wplane, qplane, lists, wt, load, send, recv, pair_send, pair_recv,
):
    x, z, core = place()
    y = lax.axis_index("group")
    chip = z * RING + x

    def turn(value, offset):
        return lax.rem(value + offset, RING)

    def slot(ox, oz):
        return turn(z, oz) * RING + turn(x, ox)

    sibling = device(x, z, 1 - core)
    loads = [
        pltpu.make_async_copy(source, target, load.at[n])
        for n, (source, target) in enumerate((
            (tok_h, tok), (gain_h, gain), (wq_h, wq), (wk_h, wk), (wv_h, wv), (wo_h, wo),
            (omap_h, omap), (pimg_h, pimg), (conf_h, conf),
        ))
    ]
    for one in loads:
        one.start()
    barrier = pltpu.get_barrier_semaphore()
    for offset in (1, 2, 3):
        for peer in (device(turn(x, offset), z, core), device(x, turn(z, offset), core), {"group": turn(y, offset)}):
            pl.semaphore_signal(barrier, 1, device_id=peer, device_id_type=MESH)
    pl.semaphore_signal(barrier, 1, device_id=sibling, device_id_type=MESH)

    for one in loads:
        one.wait()
    values = tok[0].astype(F32)
    centred = values - jnp.mean(values, axis=-1, keepdims=True)
    variance = jnp.mean(centred * centred, axis=-1, keepdims=True)
    img[chip] = (centred * lax.rsqrt(variance + 1e-05) * gain[...].reshape(1, D)).astype(BF16)

    square = (lax.broadcasted_iota(I32, (32, 32), 0), lax.broadcasted_iota(I32, (32, 32), 1))
    owners = jnp.sum(jnp.where(square[0] == square[1], omap[...], 0), axis=1, keepdims=True)
    image = lax.broadcasted_iota(I32, (32, 8), 0)
    stored = [
        jnp.sum(jnp.where(pimg[r:r + 1, :] == image, owners, 0), axis=0, keepdims=True) for r in (0, 1)
    ]
    listed = lax.broadcasted_iota(I32, (2, 8), 1) < pcnt[...]
    entries = jnp.concatenate(stored + [jnp.where(listed, conf[...], 0), jnp.zeros((4, 8), I32)], axis=0)
    entries = jnp.concatenate([entries, jnp.zeros((8, 120), I32)], axis=1)
    lists[core, chip] = pltpu.roll(entries, 8 * chip, 1)

    @pl.when(x == y)
    def _():
        keys, values, queries = [w[...].astype(F32) for w in (wk, wv, wq)]
        for g in range(RING):
            low, high = g * WIDE, (g + 1) * WIDE
            staged[g] = jnp.concatenate([keys[:, low:high], values[:, low:high]], axis=1).astype(BF16)
            staged_query[g] = jnp.concatenate(
                [queries[:, low:high], jnp.zeros((ROWS, 64), F32)], axis=1
            ).astype(BF16)
        wplane[core, y, z] = staged[x]
        qplane[core, y, z] = staged_query[x]

    @pl.when(z == y)
    def _():
        woplane[core, y, x] = wo[...]

    pl.semaphore_wait(barrier, 10)

    started = []

    def copy(source, target, number, where):
        return pltpu.make_async_remote_copy(
            src_ref=source, dst_ref=target, send_sem=send.at[number], recv_sem=recv.at[number],
            device_id=where, device_id_type=MESH,
        )

    def start(source, target, number, where):
        one = copy(source, target, number, where)
        one.start()
        started.append(one)

    def arrived(target, number):
        copy(target, target, number, sibling).wait_recv()

    def lists_x(base):
        for offset in (1, 2, 3):
            block = lists.at[core, chip]
            start(block, block, base + offset - 1, device(turn(x, offset), z, core))

    def lists_z(base):
        for offset in (1, 2, 3):
            arrived(lists.at[core, z * RING + turn(x, 4 - offset)], base + offset - 1)
        row = lists.at[core, pl.ds(z * RING, RING)]
        for offset in (1, 2, 3):
            start(row, row, base + 2 + offset, device(x, turn(z, offset), core))

    def lists_across(base):
        for offset in (1, 2, 3):
            arrived(lists.at[core, pl.ds(turn(z, 4 - offset) * RING, RING)], base + 2 + offset)
        start(lists.at[core], lists.at[core], base + 6, sibling)

    def along(axis, offset):
        return device(turn(x, offset), z, core) if axis == 0 else device(x, turn(z, offset), core)

    def rows_first(buffer, base, outgoing, axis):
        here, there = (x, z) if axis == 0 else (z, x)
        block = buffer.at[core, y, there]

        @pl.when(here == y)
        def _():
            for offset in (1, 2, 3):
                source = block if outgoing is None else outgoing.at[turn(here, offset)]
                copy(source, block, base + offset - 1, along(axis, offset)).start()

    def rows_first_sent(buffer, base, axis):
        here, there = (x, z) if axis == 0 else (z, x)

        @pl.when(here == y)
        def _():
            for offset in (1, 2, 3):
                copy(buffer.at[core, y, there], buffer.at[core, y, there], base + offset - 1, sibling).wait_send()

    def rows_second(buffer, base, axis):
        here, there = (x, z) if axis == 0 else (z, x)
        block = buffer.at[core, y, there]

        @pl.when(here != y)
        def _():
            arrived(block, base + turn(here, 4 - y) - 1)

        for offset in (1, 2, 3):
            start(block, block, base + 2 + offset, along(1 - axis, offset))

    def rows_y(buffer, base, axis):
        there = z if axis == 0 else x
        for offset in (1, 2, 3):
            arrived(buffer.at[core, y, turn(there, 4 - offset)], base + 2 + offset)
        for offset in (1, 2, 3):
            block = buffer.at[core, y]
            start(block, block, base + 5 + offset, {"group": turn(y, offset)})

    def rows_across(buffer, base):
        for offset in (1, 2, 3):
            arrived(buffer.at[core, turn(y, 4 - offset)], base + 5 + offset)
        start(buffer.at[core], buffer.at[core], base + 9, sibling)

    def ended(buffer, number):
        arrived(buffer.at[1 - core], number)

    def piece(ring, offset, half, part=None):
        low, count = (96 * half, 96) if part is None else (96 * half + 48 * part, 48)
        where = (slot(offset, 0), slot(0, offset), slot(offset, 2))[ring]
        return img.at[where, pl.ds(low, count)]

    def ring_send(ring, offset, half, part, direction, number):
        step = (1, 3)[direction]
        peer = device(x, turn(z, step), core) if ring == 1 else device(turn(x, step), z, core)
        block = piece(ring, offset, half, part)
        start(block, block, 8 * ring + 4 * half + number + direction, peer)

    def ring_start(ring, half):
        for direction in (0, 1):
            ring_send(ring, 0, half, None, direction, 0)

    def ring_pass(ring, half):
        for direction in (0, 1):
            arrived(piece(ring, (3, 1)[direction], half), 8 * ring + 4 * half + direction)
            ring_send(ring, (3, 1)[direction], half, direction, direction, 2)

    def ring_end(ring, half):
        for direction in (0, 1):
            arrived(piece(ring, 2, half, direction), 8 * ring + 4 * half + 2 + direction)

    def pair_copy(where, row):
        return pltpu.make_async_remote_copy(
            src_ref=kv.at[row], dst_ref=kv.at[row], send_sem=pair_send.at[where],
            recv_sem=pair_recv.at[where], device_id=sibling, device_id_type=MESH,
        )

    def projected(where):
        normed = img[where]
        keys = lax.dot_general(normed, wt[0:WIDE, :], NT, preferred_element_type=F32)
        values = lax.dot_general(wt[WIDE:2 * WIDE, :], normed, NT, preferred_element_type=F32)
        kv[where * 2 + core, 0:WIDE, :] = keys.astype(BF16)
        kv[where * 2 + core, WIDE:2 * WIDE, :] = values.astype(BF16)
        pair_copy(where, where * 2 + core).start()
        return keys, values

    def project(count, offsets):
        def one(i, carried):
            projected(slot(*offsets(i)))
            return carried

        lax.fori_loop(0, count, one, 0)

    def project_and_pass(k):
        keys, values = projected(slot(FIRST[k], 0))
        passed[k - 2, 0:WIDE, :] = keys[:, 0:128].astype(BF16)
        passed[k - 2, WIDE:2 * WIDE, :] = values[:, 0:128].astype(BF16)
        passed[k - 2, 2 * WIDE:3 * WIDE, :] = jnp.concatenate(
            [keys[:, 128:WIDE], values[:, 128:WIDE]], axis=1
        ).astype(BF16)
        for direction in (0, 1):
            start(
                passed.at[k - 2], taken.at[direction, k - 2], 22 + 2 * k + direction,
                device(x, turn(z, (1, 3)[direction]), core),
            )

    def tokens_pass(k):
        block = img.at[slot(FIRST[k], 0)]
        for direction in (0, 1):
            start(block, block, 22 + 2 * k + direction, device(x, turn(z, (1, 3)[direction]), core))

    def tokens_end(k):
        for direction in (0, 1):
            arrived(img.at[slot(FIRST[k], (3, 1)[direction])], 22 + 2 * k + direction)

    def take(k):
        for direction in (0, 1):
            block = taken.at[direction, k - 2]
            arrived(block, 22 + 2 * k + direction)
            where = slot(FIRST[k], (3, 1)[direction])
            row = where * 2 + core
            kv[row, :, 0:128] = block[0:2 * WIDE, :]
            rest = block[2 * WIDE:3 * WIDE, :].astype(F32)
            kv[row, 0:WIDE, 128:WIDE] = rest[:, 0:64].astype(BF16)
            kv[row, WIDE:2 * WIDE, 128:WIDE] = rest[:, 64:128].astype(BF16)
            pair_copy(where, row).start()

    W0, L0, O0, Q0 = 30, 40, 47, 57
    rows_first(wplane, W0, staged, 0)
    rows_first(qplane, Q0, staged_query, 0)
    lists_x(L0)
    ring_start(0, 0)
    ring_start(1, 0)
    ring_start(0, 1)
    rows_first(woplane, O0, None, 1)
    rows_second(wplane, W0, 0)
    ring_start(1, 1)
    rows_second(qplane, Q0, 0)
    lists_z(L0)
    ring_pass(0, 0)
    ring_pass(1, 0)
    rows_second(woplane, O0, 1)
    rows_y(wplane, W0, 0)
    ring_pass(1, 1)
    ring_pass(0, 1)
    tokens_pass(1)
    ring_end(1, 0)
    ring_start(2, 0)
    rows_across(wplane, W0)
    rows_y(qplane, Q0, 0)
    ring_end(1, 1)
    ring_start(2, 1)
    lists_across(L0)
    rows_y(woplane, O0, 1)
    ended(lists, L0 + 6)

    tables = [jnp.sum(lists[c], axis=0) for c in (0, 1)]
    attended = lax.broadcasted_iota(I32, (32, 128), 0)

    def weight_column(querying):
        taken = jnp.zeros((32, 128), I32)
        for table in tables:
            for here, there in ((0, 1), (1, 0)):
                given = jnp.where(table[here:here + 1, :] == querying, table[2 + here:3 + here, :], 0)
                taken = taken + jnp.where(table[there:there + 1, :] == attended, given, 0)
        return jnp.sum(taken, axis=1, keepdims=True)

    column = lax.broadcasted_iota(I32, (32, 128), 1)
    by_query = [weight_column((z * RING + i) * 2 + core) for i in range(RING)]
    used = jnp.zeros((32, 128), F32)
    for i in range(RING):
        used = jnp.where((column == i) & (by_query[i] > 0), 1.0, used)
    above = jnp.where(square[1] < square[0], 1.0, 0.0)
    before = jnp.dot(above.astype(BF16), used.astype(BF16), preferred_element_type=F32)
    in_column = jnp.sum(used, axis=0, keepdims=True)
    first = jnp.zeros((1, 1), F32)
    numbers, amounts = jnp.zeros((32, 128), I32), jnp.zeros((32, 128), I32)
    for i in range(RING):
        rank = (before[:, i:i + 1] + first).astype(I32)
        here = jnp.where(by_query[i] > 0, rank, -1) == column
        numbers = numbers + jnp.where(here, attended * RING + i, 0)
        amounts = amounts + jnp.where(here, by_query[i], 0)
        first = first + in_column[:, i:i + 1]
    directions[0:1, :] = jnp.sum(numbers, axis=0, keepdims=True)
    directions[1:2, :] = jnp.sum(amounts, axis=0, keepdims=True)
    directions[2:3, :] = jnp.broadcast_to(first.astype(I32), (1, 128))
    directions[3:8, :] = jnp.zeros((5, 128), I32)
    own = jnp.sum(weight_column(chip * 2 + core).astype(F32), axis=0, keepdims=True)
    total[...] = jnp.broadcast_to(1.0 + own, (8, 128))

    ended(wplane, W0 + 9)

    for j in (0, 1):
        wt[0:2 * WIDE, 384 * j:384 * (j + 1)] = in_order([wplane.at[0], wplane.at[1]], j).T.astype(BF16)
    project_and_pass(2)
    ring_end(0, 0)
    ring_end(0, 1)
    project_and_pass(3)
    rows_across(qplane, Q0)
    project(4, lambda i: (0, i))
    project(1, lambda i: (i + 3, i))

    ring_pass(2, 0)
    ended(qplane, Q0 + 9)
    for j in (0, 1):
        wt[2 * WIDE:2 * WIDE + 256, 384 * j:384 * (j + 1)] = in_order([qplane.at[0], qplane.at[1]], j).T.astype(BF16)

    def one_query(i, carried):
        query = lax.dot_general(
            wt[2 * WIDE:3 * WIDE, :], img[z * RING + i], NT, preferred_element_type=F32
        ).astype(BF16)
        both[i] = jnp.zeros((128, 2 * SEQ), BF16)
        for h in (0, 1):
            both[i, 64 * h:64 * (h + 1), SEQ * h:SEQ * (h + 1)] = query[64 * h:64 * (h + 1), :]
        third[i] = query[128:192, :]
        return carried

    lax.fori_loop(0, RING, one_query, 0)
    tokens_end(1)
    project(2, lambda i: (i * 0 + 3, 1 + 2 * i))
    ring_pass(2, 1)
    project(2, lambda i: (1 + 2 * i, 2))
    take(2)
    take(3)
    ring_end(2, 0)
    ring_end(2, 1)
    project(1, lambda i: (i + 2, i + 2))

    for offset in (1, 2, 3):
        arrived(woplane.at[core, turn(y, 4 - offset)], O0 + 5 + offset)
    for one in started:
        one.wait_send()
    rows_first_sent(wplane, W0, 0)
    rows_first_sent(qplane, Q0, 0)
    rows_first_sent(woplane, O0, 1)

    def drain(where, carried):
        pair_copy(where, where * 2 + core).wait_send()
        pair_copy(where, where * 2 + 1 - core).wait_recv()
        return carried

    lax.fori_loop(0, PLANE, drain, 0)


WINDOWS = ((0, 256, 0), (128, 384, 64), (0, 192, 0))
TOGETHER = 6


def attend_kernel(directions, kv, both, third, out, acc):
    acc[...] = jnp.zeros_like(acc)
    count = directions[2, 0]
    factor = math.log2(math.e) / 8.0

    def attention(scores):
        top = jnp.max(scores, axis=0, keepdims=True)
        expo = jnp.exp2((scores - top) * factor)
        return expo.astype(BF16), 1.0 / jnp.sum(expo, axis=0, keepdims=True)

    def several(step, carried):
        entries = [TOGETHER * step + part for part in range(TOGETHER)]
        places = [(directions[0, entry] // RING, directions[0, entry] % RING) for entry in entries]
        given = [directions[1, entry].astype(F32) for entry in entries]
        scores = [
            (
                jnp.dot(kv[t, 0:WIDE, 0:128], both[i], preferred_element_type=F32),
                jnp.dot(kv[t, 0:WIDE, 128:192], third[i], preferred_element_type=F32),
            )
            for t, i in places
        ]
        shares = [[attention(part) for part in one] for one in scores]
        found = []
        for (t, _), share, weight in zip(places, shares, given):
            for h, (low, high, _) in enumerate(WINDOWS):
                expo, scale = share[h // 2]
                one = jnp.dot(
                    kv[t, WIDE + 64 * h:WIDE + 64 * (h + 1), :], expo[:, low:high],
                    preferred_element_type=F32,
                )
                found.append((one * scale[:, low:high]).astype(BF16).astype(F32) * weight)
        for n, (_, i) in enumerate(places):
            for h in range(3):
                one = found[3 * n + h]
                acc[i, h, :, 0:one.shape[1]] += one
        return carried

    lax.fori_loop(0, (count + TOGETHER - 1) // TOGETHER, several, 0)
    for i in range(RING):
        heads = [acc[i, h][:, low:low + SEQ] for h, (_, _, low) in enumerate(WINDOWS)]
        summed = jnp.concatenate(heads, axis=0).astype(BF16)
        out[i, 0:WIDE, :] = summed[:, 0:128]
        out[i, WIDE:WIDE + 96, :] = jnp.concatenate([summed[0:96, 128:192], summed[96:192, 128:192]], axis=1)


def output_kernel(attended, woplane, total, out, wo_all, wo_both, held, send, recv):
    x, z, core = place()
    sibling = device(x, z, 1 - core)
    barrier = pltpu.get_barrier_semaphore()
    for offset in (1, 2, 3):
        pl.semaphore_signal(
            barrier, 1, device_id=device(lax.rem(x + offset, RING), z, core), device_id_type=MESH
        )
    pl.semaphore_signal(barrier, 1, device_id=sibling, device_id_type=MESH)
    pl.semaphore_wait(barrier, 4)
    copies = []
    for offset in (2, 1, 3):
        peer = lax.rem(x + offset, RING)
        one = pltpu.make_async_remote_copy(
            src_ref=attended.at[peer], dst_ref=held.at[x], send_sem=send.at[offset - 1],
            recv_sem=recv.at[offset - 1], device_id=device(peer, z, core), device_id_type=MESH,
        )
        one.start()
        copies.append(one)

    across = pltpu.make_async_remote_copy(
        src_ref=woplane.at[core], dst_ref=wo_both.at[core], send_sem=send.at[3], recv_sem=recv.at[3],
        device_id=sibling, device_id_type=MESH,
    )
    across.start()
    copies.append(across)
    wo_both[core] = woplane[core]
    pltpu.make_async_remote_copy(
        src_ref=woplane.at[core], dst_ref=wo_both.at[1 - core], send_sem=send.at[3], recv_sem=recv.at[3],
        device_id=sibling, device_id_type=MESH,
    ).wait_recv()
    for j in (0, 1):
        wo_all[384 * j:384 * (j + 1), :] = in_order([wo_both.at[0], wo_both.at[1]], j, True).astype(BF16)

    def product(peer, block):
        summed = jnp.concatenate(
            [block[0:WIDE, :], jnp.concatenate([block[WIDE:, 0:64], block[WIDE:, 64:128]], axis=0)], axis=1
        )
        rows = pl.ds(pl.multiple_of(peer * WIDE, WIDE), WIDE)
        return lax.dot_general(summed, wo_all[rows, :], TN, preferred_element_type=F32)

    numerator = product(x, attended[x])
    for offset in (1, 3, 2):
        peer = lax.rem(x + 4 - offset, RING)
        pltpu.make_async_remote_copy(
            src_ref=attended.at[peer], dst_ref=held.at[peer], send_sem=send.at[offset - 1],
            recv_sem=recv.at[offset - 1], device_id=device(peer, z, core), device_id_type=MESH,
        ).wait_recv()
        numerator += product(peer, held[peer])
    out[0] = (numerator * (1.0 / total[0:1, 0:1])).astype(BF16)
    for one in copies:
        one.wait_send()


VMEM = pl.BlockSpec(memory_space=pltpu.VMEM)
SMEM = pl.BlockSpec(memory_space=pltpu.SMEM)
HBM = pl.BlockSpec(memory_space=pltpu.HBM)


def shards(tokens, norm_gain, w_query, w_key, w_value, w_out, owner_map, pair_images, pair_count, confidence):
    kv, both, third, directions, total, woplane = pl.pallas_call(
        gather_kernel,
        out_shape=(
            jax.ShapeDtypeStruct((2 * PLANE, 2 * WIDE, SEQ), BF16),
            jax.ShapeDtypeStruct((RING, 128, 2 * SEQ), BF16),
            jax.ShapeDtypeStruct((RING, 64, SEQ), BF16),
            jax.ShapeDtypeStruct((8, 128), I32),
            jax.ShapeDtypeStruct((8, 128), F32),
            jax.ShapeDtypeStruct((2, RING, RING, ROWS, D), BF16),
        ),
        in_specs=[HBM] * 8 + [VMEM, HBM],
        out_specs=(VMEM,) * 6,
        scratch_shapes=[
            pltpu.VMEM((1, SEQ, D), BF16),
            pltpu.VMEM((D,), F32),
            pltpu.VMEM((ROWS, D), BF16),
            pltpu.VMEM((ROWS, D), BF16),
            pltpu.VMEM((ROWS, D), BF16),
            pltpu.VMEM((ROWS, D), BF16),
            pltpu.VMEM((1, 32), I32),
            pltpu.VMEM((2, 8), I32),
            pltpu.VMEM((2, 8), I32),
            pltpu.VMEM((PLANE, SEQ, D), BF16),
            pltpu.VMEM((2, 3 * WIDE, 128), BF16),
            pltpu.VMEM((2, 2, 3 * WIDE, 128), BF16),
            pltpu.VMEM((RING, ROWS, 2 * WIDE), BF16),
            pltpu.VMEM((RING, ROWS, 256), BF16),
            pltpu.VMEM((2, RING, RING, ROWS, 2 * WIDE), BF16),
            pltpu.VMEM((2, RING, RING, ROWS, 256), BF16),
            pltpu.VMEM((2, PLANE, 8, 128), I32),
            pltpu.VMEM((640, D), BF16),
            pltpu.SemaphoreType.DMA((9,)),
            pltpu.SemaphoreType.DMA((67,)),
            pltpu.SemaphoreType.DMA((67,)),
            pltpu.SemaphoreType.DMA((PLANE,)),
            pltpu.SemaphoreType.DMA((PLANE,)),
        ],
        compiler_params=pltpu.CompilerParams(
            collective_id=0, has_side_effects=True, vmem_limit_bytes=32 * 1024 * 1024
        ),
        name="gather_project",
    )(
        *[
            pltpu.with_memory_space_constraint(one, pltpu.HBM)
            for one in (tokens, norm_gain, w_query, w_key, w_value, w_out, owner_map, pair_images.T)
        ],
        pair_count.reshape(1, 1), pltpu.with_memory_space_constraint(confidence.T, pltpu.HBM),
    )
    attended = pl.pallas_call(
        attend_kernel,
        out_shape=jax.ShapeDtypeStruct((RING, WIDE + 96, 128), BF16),
        in_specs=[SMEM, VMEM, VMEM, VMEM],
        out_specs=VMEM,
        scratch_shapes=[
            pltpu.VMEM((RING, 3, 64, 256), F32),
        ],
        compiler_params=pltpu.CompilerParams(vmem_limit_bytes=32 * 1024 * 1024),
        name="attend",
    )(directions, kv, both, third)
    return pl.pallas_call(
        output_kernel,
        out_shape=jax.ShapeDtypeStruct((1, SEQ, D), BF16),
        in_specs=[VMEM] * 3,
        out_specs=VMEM,
        scratch_shapes=[
            pltpu.VMEM((D, D), BF16),
            pltpu.VMEM((2, RING, RING, ROWS, D), BF16),
            pltpu.VMEM((RING, WIDE + 96, 128), BF16),
            pltpu.SemaphoreType.DMA((4,)),
            pltpu.SemaphoreType.DMA((4,)),
        ],
        compiler_params=pltpu.CompilerParams(
            collective_id=1, has_side_effects=True, vmem_limit_bytes=32 * 1024 * 1024
        ),
        name="exchange_output",
    )(attended, woplane, total)


def solution(mesh):
    both = P(("group", "shard"))
    in_specs = (
        P(("group", "shard"), None, None),
        P(),
        P("shard", None),
        P("shard", None),
        P("shard", None),
        P("shard", None),
        P("group", None),
        P(("group", "shard"), None),
        both,
        P(("group", "shard"), None),
    )
    out_specs = P(("group", "shard"), None, None)
    return jax.shard_map(shards, mesh=mesh, in_specs=in_specs, out_specs=out_specs, check_vma=False)
```
